128 devices in a mesh: pts: 128 (over x, z, y, core).
Axes of the slice: x: 4, y: 4, z: 4, core: 2. Of those that a mesh axis runs over, the one named last changes fastest.
Arguments:
- positions: float32 [3, 1048576], P(None, 'pts'), as said below
- noise: float32 [1048576], P('pts'), may hold values from 1 to 4
- right_side: float32 [32, 1048576], P(None, 'pts')
- pairs: int32 [2, 131072], P(None, 'pts'), may hold values from 0 to 8191, as said below
- counts: int32 [128], P('pts'), may hold values from 64 to 1024, as said below
Outputs:
- solution_field: float32 [32, 1048576], P(None, 'pts')
- residual: float32 [32, 1048576], P(None, 'pts')
The draws below stay inside these ranges and needn't reach their ends.
Inputs may be any that keep to these rules, and one draw needn't show every extreme that they name: `pairs`: device d's slots are d * 1024 to (d + 1) * 1024 - 1. In every slot the row block is one of the 64 blocks device d holds. In a used slot the column block lies 0 to 15 blocks after the row block; used slots come in non-decreasing order of row block, every block's pair with itself is used, and no pair is used twice. Unused slots name a block of device d twice. counts[d] is the number of used slots of device d; some device uses all 1024. `positions`: points of two blocks that no used slot pairs are one unit or more apart.
All inputs are finite; a program needn't handle non-finite values.
Results may differ from the reference program's by a relative error of at most 0.0004.
Values sent between devices are 32-bit elements; how exact they have to be, the bound alone decides.
A program may use at most 64 MiB of HBM per device.

```python
import math
import jax
import jax.numpy as jnp
from jax import lax

BLK = 128
BLK_DEV = 64
REACH = 15
FRAMES = 32
ITERS = 2
PAIR_DEV = 1024
NPTS = 1048576
N_PTS = 128


def chain_centres(key):
    gap_key = jax.random.fold_in(key, 101)
    full_key = jax.random.fold_in(key, 102)
    nblocks = BLK_DEV * N_PTS
    gaps = jax.random.randint(gap_key, (nblocks,), 1, 4)
    full_dev = jax.random.randint(full_key, (), 0, N_PTS - 1)
    index = jnp.arange(nblocks, dtype=jnp.int32)
    lower = full_dev * BLK_DEV
    upper = (full_dev + 1) * BLK_DEV + REACH
    gaps = jnp.where((index > lower) & (index <= upper), 1, gaps)
    gaps = jnp.where((index > 0) & (index % BLK_DEV < REACH), 1, gaps)
    return jnp.cumsum(gaps).astype(jnp.int32)


def pair_table(key):
    centres = chain_centres(key)
    nblocks = BLK_DEV * N_PTS
    rows = jnp.repeat(jnp.arange(nblocks, dtype=jnp.int32), REACH + 1)
    offsets = jnp.tile(jnp.arange(REACH + 1, dtype=jnp.int32), nblocks)
    cols = rows + offsets
    safe_cols = jnp.minimum(cols, nblocks - 1)
    used = (cols < nblocks) & (centres[safe_cols] - centres[rows] <= REACH)
    used = used.reshape(N_PTS, PAIR_DEV)
    rows = rows.reshape(N_PTS, PAIR_DEV)
    cols = cols.reshape(N_PTS, PAIR_DEV)
    order = jnp.argsort(1 - used.astype(jnp.int32), axis=1, stable=True)
    used_sorted = jnp.take_along_axis(used, order, axis=1)
    rows_sorted = jnp.take_along_axis(rows, order, axis=1)
    cols_sorted = jnp.where(used_sorted, jnp.take_along_axis(cols, order, axis=1), rows_sorted)
    table = jnp.stack([rows_sorted.reshape(-1), cols_sorted.reshape(-1)]).astype(jnp.int32)
    return (table, jnp.sum(used.astype(jnp.int32), axis=1).astype(jnp.int32))


def draw_pairs(key, part):
    table, amounts = pair_table(key)
    return table


def draw_counts(key, part):
    table, amounts = pair_table(key)
    return amounts


def draw_positions(key, part):
    centres = chain_centres(key)
    key = jax.random.fold_in(key, 7)
    lift_key, wide_key, depth_key = jax.random.split(key, 3)
    npoints = BLK_DEV * N_PTS * BLK
    span = REACH + 1
    half_span = max(span // 2, 1)
    cluster = (centres // span).astype(jnp.float32)
    shelf = (centres // half_span % 2).astype(jnp.float32)
    thick = 0.25
    lift = jnp.repeat(cluster * (1.02 + thick), BLK) + jax.random.uniform(lift_key, (npoints,), jnp.float32, 0.0, thick)
    across = jnp.repeat(0.9 * shelf, BLK) + jax.random.uniform(wide_key, (npoints,), jnp.float32, -0.6, 0.6)
    depth = 2.0 * span
    deep = jax.random.uniform(depth_key, (npoints,), jnp.float32, 0.0, depth)
    return jnp.stack([across, lift, deep], axis=0).astype(jnp.float32)


def draw_right_side(key, part):
    key = jax.random.fold_in(key, 11)
    frame_key, rough_key, base_key = jax.random.split(key, 3)
    npoints = BLK_DEV * N_PTS * BLK
    frame_scale = jnp.exp(jax.random.uniform(frame_key, (FRAMES, 1), jnp.float32, 0.0, math.log(10.0))) / 3.0
    rise = jnp.exp(math.log(3.0) * jnp.arange(npoints, dtype=jnp.float32) / (npoints - 1))
    rough = jnp.exp(jax.random.uniform(rough_key, (1, npoints), jnp.float32, math.log(0.5), math.log(2.0)))
    base = jax.random.normal(base_key, (FRAMES, npoints), jnp.float32)
    return (2.0 * base * frame_scale * rise[None, :] * rough).astype(jnp.float32)


def shard_levels(key, dims, pieces, least, top_value):
    loudness, own = 1.0, jax.random.fold_in(key, 6)
    for axis_at, parts in pieces:
        draws = jnp.exp(jax.random.uniform(jax.random.fold_in(own, axis_at), (parts,), jnp.float32, least / len(pieces), top_value / len(pieces)))
        loudness = loudness * jnp.repeat(draws, dims[axis_at] // parts).reshape([-1 if axis == axis_at else 1 for axis in range(len(dims))])
    return loudness


def setup_inputs(seed: int = 0) -> dict:
    key_of = jax.random.split(jax.random.key(seed), 6)
    return {
        "positions": draw_positions(jax.random.fold_in(key_of[5], 71), 0),
        "noise": jnp.clip(jnp.exp(math.log(4.0) - 1.3862944 * jax.random.uniform(key_of[1], (NPTS,), jnp.float32) ** shard_levels(key_of[1], (NPTS,), ((0, 128),), -0.2, 0.2)), 1.0, 4.0),
        "right_side": draw_right_side(jax.random.fold_in(key_of[5], 71), 0),
        "pairs": draw_pairs(jax.random.fold_in(key_of[5], 71), 0),
        "counts": draw_counts(jax.random.fold_in(key_of[5], 71), 0),
    }


def wendland(left, right):
    diff = left[:, :, :, None] - right[:, :, None, :]
    dist = jnp.sqrt(lax.optimization_barrier(jnp.sum(diff * diff, axis=1)))
    reach = jnp.maximum(1.0 - dist, 0.0)
    return reach * reach * (reach * reach) * (4.0 * dist + 1.0)

def reference(positions, noise, right_side, pairs, counts):
    nblocks = NPTS // BLK
    pos_blocks = positions.reshape(3, nblocks, BLK).transpose(1, 0, 2)
    slot_ids = jnp.arange(PAIR_DEV, dtype=jnp.int32)

    def apply(values):
        val_blocks = values.reshape(FRAMES, nblocks, BLK).transpose(1, 0, 2)

        def step(total, device):
            chosen = lax.dynamic_slice_in_dim(pairs, (device * PAIR_DEV).astype(jnp.int32), PAIR_DEV, 1)
            rows, cols = (chosen[0], chosen[1])
            live = (slot_ids < counts[device]).astype(jnp.float32)
            cross = live * (rows != cols).astype(jnp.float32)
            kern = wendland(pos_blocks[rows], pos_blocks[cols])
            front = jnp.einsum('gij,gfj->gfi', kern, val_blocks[cols], precision=lax.Precision.HIGHEST)
            back = jnp.einsum('gij,gfi->gfj', kern, val_blocks[rows], precision=lax.Precision.HIGHEST)
            total = total.at[rows].add(front * live[:, None, None])
            total = total.at[cols].add(back * cross[:, None, None])
            return (total, None)
        total, _ = lax.scan(step, jnp.zeros(val_blocks.shape, jnp.float32), jnp.arange(N_PTS, dtype=jnp.int32))
        return total.transpose(1, 0, 2).reshape(FRAMES, NPTS) + noise[None, :] * values
    solution_field = jnp.zeros_like(right_side)
    residual = right_side
    direction = right_side
    norm_now = lax.optimization_barrier(jnp.sum(residual * residual, axis=1))
    for step_index in range(ITERS):
        image = apply(direction)
        alpha = norm_now / lax.optimization_barrier(jnp.sum(direction * image, axis=1))
        solution_field = solution_field + alpha[:, None] * direction
        residual = residual - alpha[:, None] * image
        norm_next = lax.optimization_barrier(jnp.sum(residual * residual, axis=1))
        direction = residual + (norm_next / norm_now)[:, None] * direction
        norm_now = norm_next
    return (solution_field, residual)
```

```python
import functools

import jax
import jax.numpy as jnp
from jax import lax
from jax.experimental import pallas as pl
from jax.experimental.pallas import tpu as pltpu
from jax.sharding import PartitionSpec as P

SUP = 256
HALO = 8
FRAMES = 32
TINY = 1e-36
MESH = pl.DeviceIdType.MESH
VMEM = pl.BlockSpec(memory_space=pltpu.VMEM)
SMEM = pl.BlockSpec(memory_space=pltpu.SMEM)
GROUP = 8


def f32(shape):
    return jax.ShapeDtypeStruct(shape, jnp.float32)


def dot(left, right, dim):
    return lax.dot_general(
        left, right, (((1,), (dim,)), ((), ())), preferred_element_type=jnp.float32
    )


def lanes(index, width=SUP):
    return pl.ds(pl.multiple_of(index * width, width), width)


def spread_rows(pos_ref, rows_ref, rows):
    def step(a, _):
        turned = jnp.transpose(pos_ref[:, lanes(a)])
        for c in range(3):
            rows_ref[a, c] = jnp.broadcast_to(turned[:, c : c + 1], (SUP, 128))
        return 0

    lax.fori_loop(0, rows, step, 0)


def split(values):
    high = values.astype(jnp.bfloat16)
    low = (values - high.astype(jnp.float32)).astype(jnp.bfloat16)
    return jnp.concatenate([high, low], axis=0)


def sweep(span_ref, pos_ref, rows_ref, vals_ref, tiles, out_ref, rows):
    total = span_ref[rows]

    def following(a, c):
        last = c >= a + span_ref[a]
        a_next = jnp.minimum(jnp.where(last, a + 1, a), rows - 1)
        return a_next, jnp.where(last, a_next, c + 1)

    def kernel_rows(a, c, into, part, parts):
        high_ref, low_ref = into
        step = 16
        for i in range(part * SUP // parts, (part + 1) * SUP // parts, step):
            for h in range(2):
                dist2 = None
                for axis in range(3):
                    col = pos_ref[axis : axis + 1, pl.ds(pl.multiple_of(c * SUP + h * 128, 128), 128)]
                    diff = rows_ref[a, axis, i : i + step, :] - col
                    dist2 = diff * diff if axis == 0 else dist2 + diff * diff
                dist2 = jnp.maximum(dist2, TINY)
                reach = jnp.maximum(1.0 - dist2 * lax.rsqrt(dist2), 0.0)
                square = reach * reach
                kern = square * square * (1.25 - reach)
                high = kern.astype(jnp.bfloat16)
                low = (kern - high.astype(jnp.float32)).astype(jnp.bfloat16)
                high_ref[i : i + step, h * 128 : (h + 1) * 128] = high
                low_ref[i : i + step, h * 128 : (h + 1) * 128] = low

    def both(now, then, tiles_now, tiles_then, valid):
        a, c = now
        high_ref, low_ref = tiles_now
        row_vals, col_vals = vals_ref[a], vals_ref[c]
        kernel_rows(*then, tiles_then, 0, 4)
        front = dot(col_vals, high_ref[...], 1)
        kernel_rows(*then, tiles_then, 1, 4)
        front += dot(col_vals, low_ref[...], 1)
        kernel_rows(*then, tiles_then, 2, 4)
        back = dot(row_vals, high_ref[...], 0)
        kernel_rows(*then, tiles_then, 3, 4)
        back += dot(row_vals, low_ref[...], 0)
        front = (front[:FRAMES] + front[FRAMES:]) * 4.0
        back = (back[:FRAMES] + back[FRAMES:]) * 4.0
        out_ref[:, lanes(a)] += jnp.where(valid, front, 0.0)
        out_ref[:, lanes(c)] += jnp.where(valid & (a != c), back, 0.0)

    def step(i, now):
        then = following(*now)
        both(now, then, tiles[0], tiles[1], True)
        later = following(*then)
        both(then, later, tiles[1], tiles[0], 2 * i + 1 < total)
        return later

    kernel_rows(0, 0, tiles[0], 0, 1)
    lax.fori_loop(0, (total + 1) // 2, step, (jnp.int32(0), jnp.int32(0)))


def lane_totals(quantities):
    stacked = jnp.concatenate(quantities + [jnp.zeros_like(quantities[0])] * (4 - len(quantities)), axis=0)
    return jnp.broadcast_to(jnp.sum(jnp.transpose(stacked), axis=0, keepdims=True), (8, 128))


def frame_columns(totals):
    turned = jnp.transpose(jnp.broadcast_to(totals, (128, 128)))
    return [turned[i * FRAMES : (i + 1) * FRAMES] for i in range(4)]


def wide(column):
    return jnp.concatenate([column, column], axis=1)


def fold(values):
    return values[:, :128] + values[:, 128:]


def first_kernel(span_ref, pos_ref, noise_ref, own_ref, halo_ref, out_ref, sums_ref, rows_ref, vals_ref, *tiles):
    rows = own_ref.shape[1] // SUP
    spread_rows(pos_ref, rows_ref, rows)
    zero = jnp.zeros((FRAMES, 128), jnp.float32)

    def begin(a, norm):
        values = own_ref[:, lanes(a)]
        vals_ref[a] = split(values)
        out_ref[:, lanes(a)] = noise_ref[:, lanes(a)] * values
        return norm + fold(values * values)

    norm = lax.fori_loop(0, rows, begin, zero)

    def begin_halo(a, _):
        vals_ref[rows + a] = split(halo_ref[:, lanes(a)])
        out_ref[:, lanes(rows + a)] = jnp.zeros((FRAMES, SUP), jnp.float32)
        return 0

    lax.fori_loop(0, HALO, begin_halo, 0)
    sweep(span_ref, pos_ref, rows_ref, vals_ref, (tiles[:2], tiles[2:]), out_ref, rows)
    curve = lax.fori_loop(0, rows, lambda a, s: s + fold(own_ref[:, lanes(a)] * out_ref[:, lanes(a)]), zero)
    curve = lax.fori_loop(
        0, HALO, lambda a, s: s + fold(halo_ref[:, lanes(a)] * out_ref[:, lanes(rows + a)]), curve
    )
    sums_ref[...] = lane_totals([norm, curve])


def second_kernel(
    span_ref, pos_ref, noise_ref, own_ref, halo_ref, image_ref, left_ref, right_ref, first_ref,
    out_ref, sums_ref, rows_ref, vals_ref, resid_ref, *tiles
):
    rows = own_ref.shape[1] // SUP
    spread_rows(pos_ref, rows_ref, rows)
    norm_before, curve_before = frame_columns(first_ref[0:1])[:2]
    alpha = wide(norm_before / curve_before)
    zero = jnp.zeros((FRAMES, 128), jnp.float32)

    def begin(a, image, values, sums):
        residual = values - alpha * image
        vals_ref[a] = split(residual)
        resid_ref[:, lanes(a)] = residual
        out_ref[:, lanes(a)] = noise_ref[:, lanes(a)] * residual
        return (sums[0] + fold(residual * residual), sums[1] + fold(residual * image))

    def begin_first(a, sums):
        return begin(a, image_ref[:, lanes(a)] + left_ref[:, lanes(a)], own_ref[:, lanes(a)], sums)

    def begin_rest(a, sums):
        return begin(a, image_ref[:, lanes(a)], own_ref[:, lanes(a)], sums)

    sums = lax.fori_loop(0, HALO, begin_first, (zero, zero))
    norm, cross = lax.fori_loop(HALO, rows, begin_rest, sums)

    def begin_halo(a, _):
        image = image_ref[:, lanes(rows + a)] + right_ref[:, lanes(a)]
        residual = halo_ref[:, lanes(a)] - alpha * image
        vals_ref[rows + a] = split(residual)
        resid_ref[:, lanes(rows + a)] = residual
        out_ref[:, lanes(rows + a)] = jnp.zeros((FRAMES, SUP), jnp.float32)
        return 0

    lax.fori_loop(0, HALO, begin_halo, 0)
    sweep(span_ref, pos_ref, rows_ref, vals_ref, (tiles[:2], tiles[2:]), out_ref, rows)
    curve = lax.fori_loop(
        0, rows + HALO, lambda a, s: s + fold(resid_ref[:, lanes(a)] * out_ref[:, lanes(a)]), zero
    )
    sums_ref[...] = lane_totals([norm, curve, cross])


def apply_call(kernel, operands, rows, with_residual):
    extent = (rows + HALO) * SUP
    scratch = [
        pltpu.VMEM((rows, 3, SUP, 128), jnp.float32),
        pltpu.VMEM((rows + HALO, 2 * FRAMES, SUP), jnp.bfloat16),
    ]
    if with_residual:
        scratch.append(pltpu.VMEM((FRAMES, extent), jnp.float32))
    scratch += [pltpu.VMEM((SUP, SUP), jnp.bfloat16)] * 4
    return pl.pallas_call(
        kernel,
        out_shape=(f32((FRAMES, extent)), f32((8, 128))),
        in_specs=[SMEM] + [VMEM] * (len(operands) - 1),
        out_specs=(VMEM, VMEM),
        scratch_shapes=scratch,
        compiler_params=pltpu.CompilerParams(vmem_limit_bytes=44 * 2**20),
    )(*operands)


def exchange_kernel(both_ways, rows, part_ref, sums_ref, *refs):
    if both_ways:
        left_out, right_out, total_out, left_buf, right_buf, near, far, mine, edge_sems, near_sems, far_sems = refs
    else:
        left_out, total_out, left_buf, near, far, mine, edge_sems, near_sems, far_sems = refs
    size = lax.axis_size("pts")
    me = lax.axis_index("pts")
    groups = size // GROUP
    spot, group = lax.rem(me, GROUP), me // GROUP
    right, left = lax.rem(me + 1, size), lax.rem(me + size - 1, size)
    near_peers = [group * GROUP + lax.rem(spot + k, GROUP) for k in range(1, GROUP)]
    far_peers = [lax.rem(group + k, groups) * GROUP + spot for k in range(1, groups)]
    barrier = pltpu.get_barrier_semaphore()
    peers = near_peers + far_peers + [left, right]
    for peer in peers:
        pl.semaphore_signal(barrier, inc=1, device_id=(peer,), device_id_type=MESH)
    pl.semaphore_wait(barrier, len(peers))

    def send(src, dst, sems, index, peer):
        copy = pltpu.make_async_remote_copy(
            src_ref=src, dst_ref=dst, send_sem=sems.at[0, index], recv_sem=sems.at[1, index],
            device_id=(peer,), device_id_type=MESH,
        )
        copy.start()
        return copy

    near_copies = [send(sums_ref, near.at[k], near_sems, k, near_peers[k - 1]) for k in range(1, GROUP)]
    width = HALO * SUP
    edges = [send(part_ref.at[:, pl.ds(rows * SUP, width)], left_buf, edge_sems, 0, right)]
    if both_ways:
        edges.append(send(part_ref.at[:, pl.ds(0, width)], right_buf, edge_sems, 1, left))
    for copy in near_copies:
        copy.wait()
    total = sums_ref[...]
    for k in range(1, GROUP):
        total = total + near[k]
    mine[...] = total
    far_copies = [send(mine, far.at[k], far_sems, k, far_peers[k - 1]) for k in range(1, groups)]
    for copy in far_copies:
        copy.wait()
    for k in range(1, groups):
        total = total + far[k]
    total_out[...] = total
    for copy in edges:
        copy.wait()
    left_out[...] = left_buf[...]
    if both_ways:
        right_out[...] = right_buf[...]


def exchange(part, sums, rows, both_ways, collective_id):
    edge = f32((FRAMES, HALO * SUP))
    edges = 2 if both_ways else 1
    groups = lax.axis_size("pts") // GROUP
    return pl.pallas_call(
        functools.partial(exchange_kernel, both_ways, rows),
        out_shape=(edge,) * edges + (f32((8, 128)),),
        in_specs=[VMEM, VMEM],
        out_specs=(VMEM,) * (edges + 1),
        scratch_shapes=[pltpu.VMEM(edge.shape, jnp.float32)] * edges
        + [
            pltpu.VMEM((GROUP, 8, 128), jnp.float32),
            pltpu.VMEM((groups, 8, 128), jnp.float32),
            pltpu.VMEM((8, 128), jnp.float32),
            pltpu.SemaphoreType.DMA((2, edges)),
            pltpu.SemaphoreType.DMA((2, GROUP)),
            pltpu.SemaphoreType.DMA((2, groups)),
        ],
        compiler_params=pltpu.CompilerParams(
            collective_id=collective_id, has_side_effects=True, vmem_limit_bytes=16 * 2**20
        ),
    )(part, sums)


def last_kernel(own_ref, image_ref, left_ref, part_ref, left2_ref, first_ref, second_ref, field_ref, resid_ref):
    norm0, curve0 = frame_columns(first_ref[0:1])[:2]
    norm1, curve1, cross1 = frame_columns(second_ref[0:1])[:3]
    beta = norm1 / norm0
    alpha0 = wide(norm0 / curve0)
    alpha1 = wide(norm1 / (curve1 + 2.0 * beta * cross1 + beta * beta * curve0))
    beta = wide(beta)
    edge = (pl.program_id(0) == 0).astype(jnp.float32)

    def step(a, _):
        at = lanes(a)
        first = own_ref[:, at]
        image = image_ref[:, at] + edge * left_ref[:, at]
        residual = first - alpha0 * image
        direction = residual + beta * first
        image_next = part_ref[:, at] + edge * left2_ref[:, at] + beta * image
        field_ref[:, at] = alpha0 * first + alpha1 * direction
        resid_ref[:, at] = residual - alpha1 * image_next
        return 0

    lax.fori_loop(0, HALO, step, 0)


def last(own, image, left, part, left2, first, second):
    width = HALO * SUP
    steps = own.shape[1] // width
    moving = pl.BlockSpec((FRAMES, width), lambda i: (0, i))
    fixed = pl.BlockSpec((FRAMES, width), lambda i: (0, 0))
    small = pl.BlockSpec((8, 128), lambda i: (0, 0))
    return pl.pallas_call(
        last_kernel,
        grid=(steps,),
        out_shape=(f32(own.shape), f32(own.shape)),
        in_specs=[moving, moving, fixed, moving, fixed, small, small],
        out_specs=(moving, moving),
    )(own, image, left, part, left2, first, second)


def spans(positions, rows):
    boxed = positions.reshape(3, rows + HALO, SUP)
    low, high = jnp.min(boxed, axis=2), jnp.max(boxed, axis=2)
    alone = lax.axis_index("pts") == lax.axis_size("pts") - 1
    limit = jnp.where(alone, rows, rows + HALO)
    index = jnp.arange(rows, dtype=jnp.int32)
    span = jnp.zeros((rows,), jnp.int32)
    for k in range(1, HALO + 1):
        gap = jnp.maximum(jnp.maximum(low[:, k : k + rows] - high[:, :rows], low[:, :rows] - high[:, k : k + rows]), 0.0)
        near = (jnp.sum(gap * gap, axis=0) < 1.0) & (index + k < limit)
        span = jnp.where(near, k, span)
    return jnp.concatenate([span, jnp.sum(span + 1, keepdims=True)])


def body(positions, noise, right_side, pairs, counts):
    rows = positions.shape[1] // SUP
    width = HALO * SUP
    size = lax.axis_size("pts")
    back = [(i + 1, i) for i in range(size - 1)]
    edge_pos = lax.ppermute(positions[:, :width], "pts", back)
    halo = lax.ppermute(right_side[:, :width], "pts", back)
    pos = jnp.concatenate([positions, edge_pos], axis=1)
    span = spans(pos, rows)
    pos = jnp.concatenate([pos, jnp.zeros((5, pos.shape[1]), jnp.float32)], axis=0)
    noise = noise.reshape(1, -1)
    image, sums = apply_call(first_kernel, (span, pos, noise, right_side, halo), rows, False)
    left, right, first = exchange(image, sums, rows, True, 0)
    part, sums = apply_call(
        second_kernel, (span, pos, noise, right_side, halo, image, left, right, first), rows, True
    )
    left2, second = exchange(part, sums, rows, False, 1)
    return last(right_side, image, left, part, left2, first, second)


def solution(mesh):
    in_specs = (P(None, "pts"), P("pts"), P(None, "pts"), P(None, "pts"), P("pts"))
    out_specs = (P(None, "pts"), P(None, "pts"))
    return jax.shard_map(body, mesh=mesh, in_specs=in_specs, out_specs=out_specs, check_vma=False)
```

```python
import functools

import jax
import jax.numpy as jnp
from jax import lax
from jax.experimental import pallas as pl
from jax.experimental.pallas import tpu as pltpu
from jax.sharding import PartitionSpec as P

SUP = 256
HALO = 8
FRAMES = 32
TINY = 1e-36
MESH = pl.DeviceIdType.MESH
VMEM = pl.BlockSpec(memory_space=pltpu.VMEM)
ANY = pl.BlockSpec(memory_space=pl.ANY)
SMEM = pl.BlockSpec(memory_space=pltpu.SMEM)
BATCH = 8
TILES = (BATCH, 2, SUP, SUP)
KEPT = 17
GROUP = 8


def f32(shape):
    return jax.ShapeDtypeStruct(shape, jnp.float32)


def dot(left, right, dim):
    return lax.dot_general(
        left, right, (((1,), (dim,)), ((), ())), preferred_element_type=jnp.float32
    )


def lanes(index, width=SUP):
    return pl.ds(pl.multiple_of(index * width, width), width)


def spread_rows(pos_ref, rows_ref, rows):
    row = lax.broadcasted_iota(jnp.int32, (32, 3 * 128), 0)
    lane = lax.broadcasted_iota(jnp.int32, (32, 3 * 128), 1)
    ones = ((row & 7) == (lane >> 7)).astype(jnp.float32).astype(jnp.bfloat16)

    def step(a, _):
        rest = pos_ref[:, lanes(a)]
        terms = []
        for _ in range(3):
            term = rest.astype(jnp.bfloat16).astype(jnp.float32)
            terms.append(term)
            rest = rest - term
        terms = jnp.concatenate(terms + [jnp.zeros_like(rest)], axis=0).astype(jnp.bfloat16)
        wide_rows = lax.dot_general(terms, ones, (((0,), (0,)), ((), ())), preferred_element_type=jnp.float32)
        for c in range(3):
            rows_ref[a, c] = wide_rows[:, c * 128 : (c + 1) * 128]
        return 0

    lax.fori_loop(0, rows, step, 0, unroll=4)


def split(values):
    values = 4.0 * values
    high = values.astype(jnp.bfloat16)
    low = (values - high.astype(jnp.float32)).astype(jnp.bfloat16)
    return jnp.concatenate([high, low], axis=0)


def follower(span_ref, base, rows):
    def following(a, c):
        last = c >= a + span_ref[a - base]
        a_next = jnp.minimum(jnp.where(last, a + 1, a), base + rows - 1)
        return a_next, jnp.where(last, a_next, c + 1)

    return following


def kernel_tile(pos_ref, rows_ref, a, c, store):
    highs, lows = [], []
    step = 16
    for i in range(0, SUP, step):
        pair = []
        for h in range(2):
            dist2 = None
            for axis in range(3):
                col = pos_ref[axis : axis + 1, pl.ds(pl.multiple_of(c * SUP + h * 128, 128), 128)]
                diff = rows_ref[a, axis, i : i + step, :] - col
                dist2 = diff * diff if axis == 0 else dist2 + diff * diff
            dist2 = jnp.maximum(dist2, TINY)
            reach = jnp.maximum(1.0 - dist2 * lax.rsqrt(dist2), 0.0)
            square = reach * reach
            kern = square * square * (1.25 - reach)
            high = kern.astype(jnp.bfloat16)
            pair.append((high, (kern - high.astype(jnp.float32)).astype(jnp.bfloat16)))
        highs.append(jnp.concatenate([p[0] for p in pair], axis=1))
        lows.append(jnp.concatenate([p[1] for p in pair], axis=1))
        store(i, step, highs[-1], lows[-1])
    return jnp.concatenate(highs, axis=0), jnp.concatenate(lows, axis=0)


def products(vals_ref, out_ref, base, a, c, high, low, valid):
    row_vals, col_vals = vals_ref[a - base], vals_ref[c - base]
    front = dot(col_vals, high, 1) + dot(col_vals, low, 1)
    back = dot(row_vals, high, 0) + dot(row_vals, low, 0)
    unused = out_ref.shape[1] // SUP - 1
    out_ref[:, lanes(jnp.where(valid, a, unused))] += front[:FRAMES] + front[FRAMES:]
    out_ref[:, lanes(jnp.where(valid & (a != c), c, unused))] += back[:FRAMES] + back[FRAMES:]


def group_count(total):
    return (total + BATCH - 1) // BATCH


def sweep(span_ref, pos_ref, rows_ref, vals_ref, out_ref, base, rows, keep_ref, stage_ref, sems):
    total = span_ref[rows]
    groups = group_count(total)
    kept = jnp.minimum(groups, keep_ref.shape[0])
    following = follower(span_ref, base, rows)

    def save(g):
        slot = lax.rem(g, 2)
        return pltpu.make_async_copy(stage_ref.at[slot], keep_ref.at[g], sems.at[slot])

    def step(g, now):
        slot = lax.rem(g, 2)

        @pl.when((g >= 2) & (g - 2 < kept))
        def _():
            save(g - 2).wait()

        for u in range(BATCH):
            a, c = now

            def store(i, step, high, low):
                stage_ref[slot, u, 0, i : i + step, :] = high
                stage_ref[slot, u, 1, i : i + step, :] = low

            high, low = kernel_tile(pos_ref, rows_ref, a - base, c - base, store)
            products(vals_ref, out_ref, base, a, c, high, low, BATCH * g + u < total)
            now = following(a, c)

        @pl.when(g < kept)
        def _():
            save(g).start()

        return now

    lax.fori_loop(0, groups, step, (jnp.int32(base), jnp.int32(base)))
    for k in (2, 1):
        g = groups - k

        @pl.when((g >= 0) & (g < kept))
        def _():
            save(g).wait()


def loader(kept, groups, keeps, stage_ref, sems):
    def load(g, do):
        slot = lax.rem(g, 2)

        @pl.when(g < kept)
        def _():
            do(pltpu.make_async_copy(keeps[0].at[g], stage_ref.at[slot], sems.at[slot]))

        @pl.when((g >= kept) & (g < groups))
        def _():
            do(pltpu.make_async_copy(keeps[1].at[g - kept], stage_ref.at[slot], sems.at[slot]))

    return load


def first_load(spans, counts, keeps, stage_ref, sems):
    kept = jnp.minimum(group_count(spans[0][counts[0]]), keeps[0].shape[0])
    groups = kept + group_count(spans[1][counts[1]])
    loader(kept, groups, keeps, stage_ref, sems)(jnp.int32(0), lambda copy: copy.start())


def sweep_again(spans, bases, counts, keeps, pos_ref, rows_ref, vals_ref, out_ref, stage_ref, sems):
    totals = [span[rows] for span, rows in zip(spans, counts)]
    kept = jnp.minimum(group_count(totals[0]), keeps[0].shape[0])
    groups = kept + group_count(totals[1])
    followers = [follower(*part) for part in zip(spans, bases, counts)]

    load = loader(kept, groups, keeps, stage_ref, sems)

    def part(index, first, end, now):
        def step(g, now):
            slot = lax.rem(g, 2)
            load(g + 1, lambda copy: copy.start())
            load(g, lambda copy: copy.wait())
            for u in range(BATCH):
                a, c = now
                valid = BATCH * (g - first) + u < totals[index]
                products(vals_ref, out_ref, 0, a, c, stage_ref[slot, u, 0], stage_ref[slot, u, 1], valid)
                now = followers[index](a, c)
            return now

        return lax.fori_loop(first, end, step, (jnp.int32(now), jnp.int32(now)))

    reached = part(0, 0, kept, bases[0])
    part(1, kept, groups, bases[1])

    @pl.when(BATCH * kept < totals[0])
    def _():
        spread_rows(pos_ref, rows_ref, counts[0])

        def step(t, now):
            a, c = now
            high, low = kernel_tile(pos_ref, rows_ref, a, c, lambda *_: None)
            products(vals_ref, out_ref, 0, a, c, high, low, True)
            return followers[0](a, c)

        lax.fori_loop(BATCH * kept, totals[0], step, reached)


def lane_totals(quantities):
    stacked = jnp.concatenate(quantities + [jnp.zeros_like(quantities[0])] * (4 - len(quantities)), axis=0)
    return jnp.broadcast_to(jnp.sum(jnp.transpose(stacked), axis=0, keepdims=True), (8, 128))


def frame_columns(totals):
    turned = jnp.transpose(jnp.broadcast_to(totals, (128, 128)))
    return [turned[i * FRAMES : (i + 1) * FRAMES] for i in range(4)]


def wide(column):
    return jnp.concatenate([column, column], axis=1)


def fold(values):
    return values[:, :128] + values[:, 128:]


def zeros():
    return jnp.zeros((FRAMES, 128), jnp.float32)


def loop(low, high, step, start):
    return lax.fori_loop(low, high, step, start, unroll=4)


def inner_kernel(span_ref, pos_ref, noise_ref, own_ref, out_ref, norm_ref, keep_ref, rows_ref, vals_ref, stage_ref, sems):
    rows = own_ref.shape[1] // SUP
    spread_rows(pos_ref, rows_ref, rows - HALO)

    def begin(a, norm):
        values = own_ref[:, lanes(a)]
        vals_ref[a] = split(values)
        out_ref[:, lanes(a)] = noise_ref[:, lanes(a)] * values
        return norm + fold(values * values)

    norm_ref[...] = loop(0, rows, begin, zeros())
    sweep(span_ref, pos_ref, rows_ref, vals_ref, out_ref, 0, rows - HALO, keep_ref, stage_ref, sems)


def outer_kernel(
    span_ref, pos_ref, own_ref, halo_ref, norm_ref, begun_ref, out_ref, sums_ref, keep_ref, rows_ref, vals_ref, stage_ref, sems
):
    rows = own_ref.shape[1] // SUP
    base = rows - HALO
    spread_rows(pos_ref, rows_ref, HALO)

    def begin(a, _):
        vals_ref[a] = split(own_ref[:, lanes(base + a)])
        vals_ref[HALO + a] = split(halo_ref[:, lanes(a)])
        out_ref[:, lanes(rows + a)] = jnp.zeros((FRAMES, SUP), jnp.float32)
        return 0

    def resume(a, _):
        out_ref[:, lanes(a)] = begun_ref[:, lanes(a)]
        return 0

    loop(0, rows, resume, 0)
    loop(0, HALO, begin, 0)
    sweep(span_ref, pos_ref, rows_ref, vals_ref, out_ref, base, HALO, keep_ref, stage_ref, sems)
    curve = loop(0, rows, lambda a, s: s + fold(own_ref[:, lanes(a)] * out_ref[:, lanes(a)]), zeros())
    curve = loop(0, HALO, lambda a, s: s + fold(halo_ref[:, lanes(a)] * out_ref[:, lanes(rows + a)]), curve)
    sums_ref[...] = lane_totals([norm_ref[...], curve])


def second_kernel(
    span_ref, outer_ref, pos_ref, noise_ref, own_ref, halo_ref, image_ref, left_ref, right_ref, first_ref, keep_ref, keep2_ref,
    out_ref, sums_ref, rows_ref, vals_ref, resid_ref, stage_ref, sems
):
    rows = own_ref.shape[1] // SUP
    spans, bases, counts = (span_ref, outer_ref), (0, rows - HALO), (rows - HALO, HALO)
    keeps = (keep_ref, keep2_ref)
    first_load(spans, counts, keeps, stage_ref, sems)
    norm_before, curve_before = frame_columns(first_ref[0:1])[:2]
    alpha = wide(norm_before / curve_before)

    def begin(a, image, values, sums):
        residual = values - alpha * image
        vals_ref[a] = split(residual)
        resid_ref[:, lanes(a)] = residual
        out_ref[:, lanes(a)] = noise_ref[:, lanes(a)] * residual
        return (sums[0] + fold(residual * residual), sums[1] + fold(residual * image))

    def begin_first(a, sums):
        return begin(a, image_ref[:, lanes(a)] + left_ref[:, lanes(a)], own_ref[:, lanes(a)], sums)

    def begin_rest(a, sums):
        return begin(a, image_ref[:, lanes(a)], own_ref[:, lanes(a)], sums)

    sums = loop(0, HALO, begin_first, (zeros(), zeros()))
    norm, cross = loop(HALO, rows, begin_rest, sums)

    def begin_halo(a, _):
        image = image_ref[:, lanes(rows + a)] + right_ref[:, lanes(a)]
        residual = halo_ref[:, lanes(a)] - alpha * image
        vals_ref[rows + a] = split(residual)
        resid_ref[:, lanes(rows + a)] = residual
        out_ref[:, lanes(rows + a)] = jnp.zeros((FRAMES, SUP), jnp.float32)
        return 0

    loop(0, HALO, begin_halo, 0)
    sweep_again(spans, bases, counts, keeps, pos_ref, rows_ref, vals_ref, out_ref, stage_ref, sems)
    curve = loop(0, rows + HALO, lambda a, s: s + fold(resid_ref[:, lanes(a)] * out_ref[:, lanes(a)]), zeros())
    sums_ref[...] = lane_totals([norm, curve, cross])


def field_scratch(rows_held, vals_held):
    return [
        pltpu.VMEM((rows_held, 3, SUP, 128), jnp.float32),
        pltpu.VMEM((vals_held, 2 * FRAMES, SUP), jnp.bfloat16),
    ]


def stage_scratch():
    return [pltpu.VMEM((2,) + TILES, jnp.bfloat16), pltpu.SemaphoreType.DMA((2,))]


def local_call(kernel, operands, out_shape, scratch, smalls, anys=0, any_outs=0):
    plain = len(operands) - smalls - anys
    return pl.pallas_call(
        kernel,
        out_shape=out_shape,
        in_specs=[SMEM] * smalls + [VMEM] * plain + [ANY] * anys,
        out_specs=(VMEM,) * (len(out_shape) - any_outs) + (ANY,) * any_outs,
        scratch_shapes=scratch,
        compiler_params=pltpu.CompilerParams(vmem_limit_bytes=44 * 2**20),
    )(*operands)


def exchange_kernel(both_ways, rows, part_ref, sums_ref, *refs):
    if both_ways:
        left_out, right_out, total_out, left_buf, right_buf, near, far, mine, edge_sems, near_sems, far_sems = refs
    else:
        left_out, total_out, left_buf, near, far, mine, edge_sems, near_sems, far_sems = refs
    size = lax.axis_size("pts")
    me = lax.axis_index("pts")
    groups = size // GROUP
    spot, group = lax.rem(me, GROUP), me // GROUP
    right, left = lax.rem(me + 1, size), lax.rem(me + size - 1, size)
    near_peers = [group * GROUP + lax.rem(spot + k, GROUP) for k in range(1, GROUP)]
    far_peers = [lax.rem(group + k, groups) * GROUP + spot for k in range(1, groups)]
    barrier = pltpu.get_barrier_semaphore()
    peers = near_peers + far_peers + [left, right]
    for peer in peers:
        pl.semaphore_signal(barrier, inc=1, device_id=(peer,), device_id_type=MESH)
    pl.semaphore_wait(barrier, len(peers))

    def send(src, dst, sems, index, peer):
        copy = pltpu.make_async_remote_copy(
            src_ref=src, dst_ref=dst, send_sem=sems.at[0, index], recv_sem=sems.at[1, index],
            device_id=(peer,), device_id_type=MESH,
        )
        copy.start()
        return copy

    near_copies = [send(sums_ref, near.at[k], near_sems, k, near_peers[k - 1]) for k in range(1, GROUP)]
    width = HALO * SUP
    edges = [send(part_ref.at[:, pl.ds(rows * SUP, width)], left_buf, edge_sems, 0, right)]
    if both_ways:
        edges.append(send(part_ref.at[:, pl.ds(0, width)], right_buf, edge_sems, 1, left))
    for copy in near_copies:
        copy.wait()
    total = sums_ref[...]
    for k in range(1, GROUP):
        total = total + near[k]
    mine[...] = total
    far_copies = [send(mine, far.at[k], far_sems, k, far_peers[k - 1]) for k in range(1, groups)]
    for copy in far_copies:
        copy.wait()
    for k in range(1, groups):
        total = total + far[k]
    total_out[...] = total
    for copy in edges:
        copy.wait()
    left_out[...] = left_buf[...]
    if both_ways:
        right_out[...] = right_buf[...]


def exchange(part, sums, rows, both_ways, collective_id):
    edge = f32((FRAMES, HALO * SUP))
    edges = 2 if both_ways else 1
    groups = lax.axis_size("pts") // GROUP
    return pl.pallas_call(
        functools.partial(exchange_kernel, both_ways, rows),
        out_shape=(edge,) * edges + (f32((8, 128)),),
        in_specs=[VMEM, VMEM],
        out_specs=(VMEM,) * (edges + 1),
        scratch_shapes=[pltpu.VMEM(edge.shape, jnp.float32)] * edges
        + [
            pltpu.VMEM((GROUP, 8, 128), jnp.float32),
            pltpu.VMEM((groups, 8, 128), jnp.float32),
            pltpu.VMEM((8, 128), jnp.float32),
            pltpu.SemaphoreType.DMA((2, edges)),
            pltpu.SemaphoreType.DMA((2, GROUP)),
            pltpu.SemaphoreType.DMA((2, groups)),
        ],
        compiler_params=pltpu.CompilerParams(
            collective_id=collective_id, has_side_effects=True, vmem_limit_bytes=16 * 2**20
        ),
    )(part, sums)


def last_kernel(
    own_ref, image_ref, left_ref, part_ref, left2_ref, first_ref, second_ref, field_out, resid_out, field_ref, resid_ref, sems
):
    norm0, curve0 = frame_columns(first_ref[0:1])[:2]
    norm1, curve1, cross1 = frame_columns(second_ref[0:1])[:3]
    beta = norm1 / norm0
    alpha0 = wide(norm0 / curve0)
    alpha1 = wide(norm1 / (curve1 + 2.0 * beta * cross1 + beta * beta * curve0))
    beta = wide(beta)
    width = HALO * SUP
    copies = []
    for part in range(own_ref.shape[1] // width):
        def step(a, _):
            at = lanes(part * HALO + a)
            first, image, image_next = own_ref[:, at], image_ref[:, at], part_ref[:, at]
            if part == 0:
                image = image + left_ref[:, at]
                image_next = image_next + left2_ref[:, at]
            residual = first - alpha0 * image
            direction = residual + beta * first
            field_ref[:, at] = alpha0 * first + alpha1 * direction
            resid_ref[:, at] = residual - alpha1 * (image_next + beta * image)
            return 0

        loop(0, HALO, step, 0)
        at = pl.ds(part * width, width)
        for index, (src, dst) in enumerate(((field_ref, field_out), (resid_ref, resid_out))):
            copies.append(pltpu.make_async_copy(src.at[:, at], dst.at[:, at], sems.at[index, part]))
            copies[-1].start()
    for copy in copies:
        copy.wait()


def spans(positions, rows, limit):
    extent = positions.shape[1] // SUP
    boxed = positions.reshape(3, extent, SUP)
    low, high = jnp.min(boxed, axis=2), jnp.max(boxed, axis=2)
    index = jnp.arange(rows, dtype=jnp.int32)
    span = jnp.zeros((rows,), jnp.int32)
    for k in range(1, HALO + 1):
        ahead = slice(k, k + rows)
        gap = jnp.maximum(jnp.maximum(low[:, ahead] - high[:, :rows], low[:, :rows] - high[:, ahead]), 0.0)
        near = (jnp.sum(gap * gap, axis=0) < 1.0) & (index + k < limit)
        span = jnp.where(near, k, span)
    return jnp.concatenate([span, jnp.sum(span + 1, keepdims=True)])


def padded(positions):
    return jnp.concatenate([positions, jnp.zeros((5, positions.shape[1]), jnp.float32)], axis=0)


def body(positions, noise, right_side, pairs, counts):
    rows = positions.shape[1] // SUP
    inner = rows - HALO
    width = HALO * SUP
    size = lax.axis_size("pts")
    back = [(i + 1, i) for i in range(size - 1)]
    edge_pos = lax.ppermute(positions[:, :width], "pts", back)
    halo = lax.ppermute(right_side[:, :width], "pts", back)
    pos = padded(positions)
    noise = noise.reshape(1, -1)
    field = f32((FRAMES, (rows + HALO + 1) * SUP))
    small = f32((FRAMES, 128))
    span = spans(positions, inner, rows)
    image, norm, keep = local_call(
        inner_kernel, (span, pos, noise, right_side),
        (field, small, jax.ShapeDtypeStruct((KEPT,) + TILES, jnp.bfloat16)),
        field_scratch(inner, rows) + stage_scratch(), 1, any_outs=1,
    )
    outer_pos = jnp.concatenate([positions[:, inner * SUP :], edge_pos], axis=1)
    alone = lax.axis_index("pts") == size - 1
    outer_span = spans(outer_pos, HALO, jnp.where(alone, HALO, 2 * HALO))
    steps = -(-HALO * (HALO + 1) // BATCH)
    image, sums, keep2 = local_call(
        outer_kernel, (outer_span, padded(outer_pos), right_side, halo, norm, image),
        (field, f32((8, 128)), jax.ShapeDtypeStruct((steps,) + TILES, jnp.bfloat16)),
        field_scratch(HALO, 2 * HALO) + stage_scratch(), 1, any_outs=1,
    )
    left, right, first = exchange(image, sums, rows, True, 0)
    part, sums = local_call(
        second_kernel,
        (span, outer_span, pos, noise, right_side, halo, image, left, right, first, keep, keep2),
        (field, f32((8, 128))),
        field_scratch(inner, rows + HALO) + [pltpu.VMEM((FRAMES, (rows + HALO) * SUP), jnp.float32)] + stage_scratch(),
        2, anys=2,
    )
    left2, second = exchange(part, sums, rows, False, 1)
    parts = rows // HALO
    return local_call(
        last_kernel, (right_side, image, left, part, left2, first, second),
        (f32(right_side.shape), f32(right_side.shape)),
        [pltpu.VMEM(right_side.shape, jnp.float32)] * 2 + [pltpu.SemaphoreType.DMA((2, parts))], 0, any_outs=2,
    )


def solution(mesh):
    in_specs = (P(None, "pts"), P("pts"), P(None, "pts"), P(None, "pts"), P("pts"))
    out_specs = (P(None, "pts"), P(None, "pts"))
    return jax.shard_map(body, mesh=mesh, in_specs=in_specs, out_specs=out_specs, check_vma=False)
```

```python
import functools

import jax
import jax.numpy as jnp
from jax import lax
from jax.experimental import pallas as pl
from jax.experimental.pallas import tpu as pltpu
from jax.sharding import PartitionSpec as P

SUP = 256
HALO = 8
FRAMES = 32
TINY = 1e-36
MESH = pl.DeviceIdType.MESH
VMEM = pl.BlockSpec(memory_space=pltpu.VMEM)
ANY = pl.BlockSpec(memory_space=pl.ANY)
SMEM = pl.BlockSpec(memory_space=pltpu.SMEM)
AHEAD = 3
BATCH = 8
EIGHT = jnp.float8_e4m3fn
UNIT = 8.0
KERNEL = UNIT**5 / 4
GROUP = 8


def f32(shape):
    return jax.ShapeDtypeStruct(shape, jnp.float32)


def dot(left, right, dim):
    return lax.dot_general(
        left, right, (((1,), (dim,)), ((), ())), preferred_element_type=jnp.float32
    )


def lanes(index, width=SUP):
    return pl.ds(pl.multiple_of(index * width, width), width)


def spread_rows(pos_ref, rows_ref, rows):
    row = lax.broadcasted_iota(jnp.int32, (32, 3 * 128), 0)
    lane = lax.broadcasted_iota(jnp.int32, (32, 3 * 128), 1)
    ones = ((row & 7) == (lane >> 7)).astype(jnp.float32).astype(jnp.bfloat16)

    def step(a, _):
        rest = pos_ref[:, lanes(a)]
        terms = []
        for _ in range(3):
            term = rest.astype(jnp.bfloat16).astype(jnp.float32)
            terms.append(term)
            rest = rest - term
        terms = jnp.concatenate(terms + [jnp.zeros_like(rest)], axis=0).astype(jnp.bfloat16)
        wide_rows = lax.dot_general(terms, ones, (((0,), (0,)), ((), ())), preferred_element_type=jnp.float32)
        for c in range(3):
            rows_ref[a, c] = wide_rows[:, c * 128 : (c + 1) * 128]
        return 0

    lax.fori_loop(0, rows, step, 0, unroll=4)


def scale_of(peak):
    peak = jnp.max(peak, axis=1, keepdims=True)
    return jnp.broadcast_to(224.0 / jnp.maximum(peak, 1e-30), (FRAMES, SUP))


def hold(vals_ref, a, values):
    high_ref, low_ref = vals_ref
    low_ref[a] = values.astype(EIGHT)
    high = values.astype(jnp.bfloat16)
    low = (values - high.astype(jnp.float32)).astype(jnp.bfloat16)
    high_ref[a] = jnp.concatenate([high, low], axis=0)


def follower(span_ref, base, rows):
    def following(a, c):
        last = c >= a + span_ref[a - base]
        a_next = jnp.minimum(jnp.where(last, a + 1, a), base + rows - 1)
        return a_next, jnp.where(last, a_next, c + 1)

    return following


def kernel_tile(pos_ref, rows_ref, a, c, high_ref, low_ref):
    highs, lows = [], []
    step = 32
    for i in range(0, SUP, step):
        pair = []
        for h in range(2):
            dist2 = None
            for axis in range(3):
                col = pos_ref[axis : axis + 1, pl.ds(pl.multiple_of(c * SUP + h * 128, 128), 128)]
                diff = rows_ref[a, axis, i : i + step, :] - col
                dist2 = diff * diff if axis == 0 else dist2 + diff * diff
            dist2 = jnp.maximum(dist2, TINY)
            reach = jnp.maximum(UNIT - dist2 * lax.rsqrt(dist2), 0.0)
            square = reach * reach
            kern = square * square * (1.25 * UNIT - reach)
            high = kern.astype(jnp.bfloat16)
            pair.append((high, (kern - high.astype(jnp.float32)).astype(EIGHT)))
        highs.append(jnp.concatenate([p[0] for p in pair], axis=1))
        lows.append(jnp.concatenate([p[1] for p in pair], axis=1))
        high_ref[i : i + step, :] = highs[-1]
        low_ref[i : i + step, :] = lows[-1]
    return jnp.concatenate(highs, axis=0), jnp.concatenate(lows, axis=0)


def products(vals_ref, out_ref, base, a, c, high, low, valid):
    high_ref, low_ref = vals_ref
    front = dot(high_ref[c - base], high, 1)
    front = front[:FRAMES] + front[FRAMES:] + dot(low_ref[c - base], low, 1)
    back = dot(high_ref[a - base], high, 0)
    back = back[:FRAMES] + back[FRAMES:] + dot(low_ref[a - base], low, 0)
    unused = out_ref.shape[1] // SUP - 1
    out_ref[:, lanes(jnp.where(valid, a, unused))] += front
    out_ref[:, lanes(jnp.where(valid & (a != c), c, unused))] += back


def group_count(total):
    return (total + BATCH - 1) // BATCH


def moves(tiles, keep, g, save):
    slot = lax.rem(g, 2)
    stages, sems = tiles
    out = []
    for index in range(2):
        here, there = stages[index].at[slot], keep[index].at[g]
        src, dst = (here, there) if save else (there, here)
        out.append(pltpu.make_async_copy(src, dst, sems.at[index, slot]))
    return out


def sweep(span_ref, pos_ref, rows_ref, vals_ref, out_ref, base, rows, keep, tiles):
    total = span_ref[rows]
    groups = group_count(total)
    following = follower(span_ref, base, rows)
    highs, lows = tiles[0]

    def step(g, now):
        slot = lax.rem(g, 2)

        @pl.when(g >= 2)
        def _():
            for copy in moves(tiles, keep, g - 2, True):
                copy.wait()

        for u in range(BATCH):
            a, c = now
            high, low = kernel_tile(pos_ref, rows_ref, a - base, c - base, highs.at[slot, u], lows.at[slot, u])
            products(vals_ref, out_ref, base, a, c, high, low, BATCH * g + u < total)
            now = following(a, c)
        for copy in moves(tiles, keep, g, True):
            copy.start()
        return now

    lax.fori_loop(0, groups, step, (jnp.int32(base), jnp.int32(base)))
    for k in (2, 1):
        @pl.when(groups >= k)
        def _():
            for copy in moves(tiles, keep, groups - k, True):
                copy.wait()


def fetch(keeps, counts, tiles, g, start):
    for part, (first, end) in enumerate(((0, counts[0]), (counts[0], counts[0] + counts[1]))):
        @pl.when((g >= first) & (g < end))
        def _():
            slot = lax.rem(g, AHEAD + 1)
            for index in range(2):
                src, dst = keeps[2 * part + index].at[g - first], tiles[0][index].at[slot]
                sem = tiles[1].at[index, slot]
                copy = pltpu.make_async_copy(src, dst, sem)
                if start:
                    copy.start()
                else:
                    copy.wait()


def sweep_again(spans, bases, rows, vals_ref, out_ref, keeps, tiles):
    totals = [span[n] for span, n in zip(spans, rows)]
    counts = [group_count(total) for total in totals]
    highs, lows = tiles[0]
    first = 0
    for part in range(2):
        following = follower(spans[part], bases[part], rows[part])

        def step(g, now, first=first, total=totals[part], following=following):
            slot = lax.rem(g, AHEAD + 1)
            fetch(keeps, counts, tiles, g + AHEAD, True)
            fetch(keeps, counts, tiles, g, False)
            for u in range(BATCH):
                a, c = now
                products(
                    vals_ref, out_ref, 0, a, c, highs[slot, u], lows[slot, u], BATCH * (g - first) + u < total
                )
                now = following(a, c)
            return now

        start = jnp.int32(bases[part])
        lax.fori_loop(first, first + counts[part], step, (start, start))
        first = first + counts[part]


def lane_totals(quantities):
    stacked = jnp.concatenate(quantities + [jnp.zeros_like(quantities[0])] * (4 - len(quantities)), axis=0)
    return jnp.broadcast_to(jnp.sum(jnp.transpose(stacked), axis=0, keepdims=True), (8, 128))


def frame_columns(totals):
    turned = jnp.transpose(jnp.broadcast_to(totals, (128, 128)))
    return [turned[i * FRAMES : (i + 1) * FRAMES] for i in range(4)]


def wide(column):
    return jnp.concatenate([column, column], axis=1)


def fold(values):
    return values[:, :128] + values[:, 128:]


def zeros():
    return jnp.zeros((FRAMES, 128), jnp.float32)


def loop(low, high, step, start):
    return lax.fori_loop(low, high, step, start, unroll=4)


def clear(out_ref, first, count):
    def step(a, _):
        out_ref[:, lanes(first + a)] = jnp.zeros((FRAMES, SUP), jnp.float32)
        return 0

    loop(0, count, step, 0)


def larger(peak, values):
    values = jnp.abs(values)
    return jnp.maximum(peak, jnp.maximum(values[:, :128], values[:, 128:]))


def inner_kernel(
    span_ref, pos_ref, noise_ref, own_ref, out_ref, norm_ref, keep_high, keep_low, rows_ref, high_ref, low_ref, *stage
):
    rows = own_ref.shape[1] // SUP
    vals_ref, tiles = (high_ref, low_ref), (stage[:2], stage[2])
    scale = scale_of(loop(0, rows, lambda a, peak: larger(peak, own_ref[:, lanes(a)]), zeros()))
    spread_rows(pos_ref, rows_ref, rows - HALO)
    clear(out_ref, 0, rows)

    def begin(a, norm):
        values = own_ref[:, lanes(a)]
        hold(vals_ref, a, scale * values)
        return norm + fold(values * values)

    norm_ref[...] = loop(0, rows, begin, zeros())
    sweep(span_ref, pos_ref, rows_ref, vals_ref, out_ref, 0, rows - HALO, (keep_high, keep_low), tiles)
    inverse = 1.0 / (KERNEL * scale)

    def finish(a, _):
        at = lanes(a)
        out_ref[:, at] = out_ref[:, at] * inverse + noise_ref[:, at] * own_ref[:, at]
        return 0

    loop(0, rows, finish, 0)


def outer_kernel(
    span_ref, pos_ref, own_ref, halo_ref, norm_ref, begun_ref, out_ref, sums_ref, keep_high, keep_low,
    rows_ref, high_ref, low_ref, *stage
):
    rows = own_ref.shape[1] // SUP
    base = rows - HALO
    vals_ref, tiles = (high_ref, low_ref), (stage[:2], stage[2])

    def peaks(a, peak):
        return larger(larger(peak, own_ref[:, lanes(base + a)]), halo_ref[:, lanes(a)])

    scale = scale_of(loop(0, HALO, peaks, zeros()))
    spread_rows(pos_ref, rows_ref, HALO)
    clear(out_ref, base, 2 * HALO)

    def begin(a, _):
        hold(vals_ref, a, scale * own_ref[:, lanes(base + a)])
        hold(vals_ref, HALO + a, scale * halo_ref[:, lanes(a)])
        return 0

    loop(0, HALO, begin, 0)
    sweep(span_ref, pos_ref, rows_ref, vals_ref, out_ref, base, HALO, (keep_high, keep_low), tiles)
    inverse = 1.0 / (KERNEL * scale)

    def rest(a, curve):
        at = lanes(a)
        image = begun_ref[:, at]
        out_ref[:, at] = image
        return curve + fold(own_ref[:, at] * image)

    def edge(a, curve):
        at = lanes(base + a)
        image = begun_ref[:, at] + out_ref[:, at] * inverse
        out_ref[:, at] = image
        curve = curve + fold(own_ref[:, at] * image)
        at = lanes(rows + a)
        image = out_ref[:, at] * inverse
        out_ref[:, at] = image
        return curve + fold(halo_ref[:, lanes(a)] * image)

    curve = loop(0, HALO, edge, loop(0, base, rest, zeros()))
    sums_ref[...] = lane_totals([norm_ref[...], curve])


def second_kernel(
    span_ref, outer_ref, noise_ref, own_ref, halo_ref, image_ref, left_ref, right_ref, first_ref, *refs
):
    keeps, (out_ref, sums_ref, high_ref, low_ref, resid_ref), stage = refs[:4], refs[4:9], refs[9:]
    vals_ref, tiles = (high_ref, low_ref), (stage[:2], stage[2])
    rows = own_ref.shape[1] // SUP
    spans, bases, counts = (span_ref, outer_ref), (0, rows - HALO), (rows - HALO, HALO)
    for g in range(AHEAD):
        fetch(keeps, [group_count(span[n]) for span, n in zip(spans, counts)], tiles, jnp.int32(g), True)
    norm_before, curve_before = frame_columns(first_ref[0:1])[:2]
    alpha = wide(norm_before / curve_before)

    def begin(a, image, values, sums):
        residual = values - alpha * image
        resid_ref[:, lanes(a)] = residual
        return (
            sums[0] + fold(residual * residual), sums[1] + fold(residual * image), larger(sums[2], residual)
        )

    def begin_first(a, sums):
        return begin(a, image_ref[:, lanes(a)] + left_ref[:, lanes(a)], own_ref[:, lanes(a)], sums)

    def begin_rest(a, sums):
        return begin(a, image_ref[:, lanes(a)], own_ref[:, lanes(a)], sums)

    sums = loop(0, HALO, begin_first, (zeros(), zeros(), zeros()))
    norm, cross, peak = loop(HALO, rows, begin_rest, sums)

    def begin_halo(a, peak):
        image = image_ref[:, lanes(rows + a)] + right_ref[:, lanes(a)]
        residual = halo_ref[:, lanes(a)] - alpha * image
        resid_ref[:, lanes(rows + a)] = residual
        return larger(peak, residual)

    scale = scale_of(loop(0, HALO, begin_halo, peak))

    def ready(a, _):
        hold(vals_ref, a, scale * resid_ref[:, lanes(a)])
        return 0

    loop(0, rows + HALO, ready, 0)
    clear(out_ref, 0, rows + HALO)
    sweep_again(spans, bases, counts, vals_ref, out_ref, keeps, tiles)
    inverse = 1.0 / (KERNEL * scale)

    def finish(a, curve):
        at = lanes(a)
        image = out_ref[:, at] * inverse + noise_ref[:, at] * resid_ref[:, at]
        out_ref[:, at] = image
        return curve + fold(resid_ref[:, at] * image)

    def finish_halo(a, curve):
        at = lanes(rows + a)
        image = out_ref[:, at] * inverse
        out_ref[:, at] = image
        return curve + fold(resid_ref[:, at] * image)

    curve = loop(0, HALO, finish_halo, loop(0, rows, finish, zeros()))
    sums_ref[...] = lane_totals([norm, curve, cross])


def vals_scratch(count):
    return [
        pltpu.VMEM((count, 2 * FRAMES, SUP), jnp.bfloat16),
        pltpu.VMEM((count, FRAMES, SUP), EIGHT),
    ]


def stage_scratch(slots):
    return [
        pltpu.VMEM((slots, BATCH, SUP, SUP), jnp.bfloat16),
        pltpu.VMEM((slots, BATCH, SUP, SUP), EIGHT),
        pltpu.SemaphoreType.DMA((2, slots)),
    ]


def kept(rows):
    steps = -(-rows * (HALO + 1) // BATCH)
    shape = (steps, BATCH, SUP, SUP)
    return jax.ShapeDtypeStruct(shape, jnp.bfloat16), jax.ShapeDtypeStruct(shape, EIGHT)


def first_pass(span, outer_span, positions, edge_pos, noise, right_side, halo):
    rows = positions.shape[1] // SUP
    inner = rows - HALO
    field = f32((FRAMES, (rows + HALO + 1) * SUP))
    spread = pltpu.VMEM((inner, 3, SUP, 128), jnp.float32)
    image, norm, *keep = local_call(
        inner_kernel, (span, padded(positions), noise, right_side), (field, f32((FRAMES, 128))) + kept(inner),
        [spread] + vals_scratch(rows) + stage_scratch(2), 1, any_outs=2,
    )
    outer_pos = padded(jnp.concatenate([positions[:, inner * SUP :], edge_pos], axis=1))
    spread = pltpu.VMEM((HALO, 3, SUP, 128), jnp.float32)
    image, sums, *keep_outer = local_call(
        outer_kernel, (outer_span, outer_pos, right_side, halo, norm, image), (field, f32((8, 128))) + kept(HALO),
        [spread] + vals_scratch(2 * HALO) + stage_scratch(2), 1, any_outs=2,
    )
    return image, sums, keep + keep_outer


def second_pass(span, outer_span, noise, right_side, halo, image, left, right, first, keeps):
    extent = right_side.shape[1] // SUP + HALO
    return local_call(
        second_kernel, (span, outer_span, noise, right_side, halo, image, left, right, first, *keeps),
        (f32((FRAMES, (extent + 1) * SUP)), f32((8, 128))),
        vals_scratch(extent) + [pltpu.VMEM((FRAMES, extent * SUP), jnp.float32)] + stage_scratch(AHEAD + 1), 2, anys=4,
    )


def local_call(kernel, operands, out_shape, scratch, smalls, anys=0, any_outs=0):
    plain = len(operands) - smalls - anys
    return pl.pallas_call(
        kernel,
        out_shape=out_shape,
        in_specs=[SMEM] * smalls + [VMEM] * plain + [ANY] * anys,
        out_specs=(VMEM,) * (len(out_shape) - any_outs) + (ANY,) * any_outs,
        scratch_shapes=scratch,
        compiler_params=pltpu.CompilerParams(vmem_limit_bytes=44 * 2**20),
    )(*operands)


def exchange_kernel(both_ways, rows, part_ref, sums_ref, *refs):
    if both_ways:
        left_out, right_out, total_out, left_buf, right_buf, near, far, mine, edge_sems, near_sems, far_sems = refs
    else:
        left_out, total_out, left_buf, near, far, mine, edge_sems, near_sems, far_sems = refs
    size = lax.axis_size("pts")
    me = lax.axis_index("pts")
    groups = size // GROUP
    spot, group = lax.rem(me, GROUP), me // GROUP
    right, left = lax.rem(me + 1, size), lax.rem(me + size - 1, size)
    near_peers = [group * GROUP + lax.rem(spot + k, GROUP) for k in range(1, GROUP)]
    far_peers = [lax.rem(group + k, groups) * GROUP + spot for k in range(1, groups)]
    barrier = pltpu.get_barrier_semaphore()
    peers = near_peers + far_peers + [left, right]
    for peer in peers:
        pl.semaphore_signal(barrier, inc=1, device_id=(peer,), device_id_type=MESH)
    pl.semaphore_wait(barrier, len(peers))

    def send(src, dst, sems, index, peer):
        copy = pltpu.make_async_remote_copy(
            src_ref=src, dst_ref=dst, send_sem=sems.at[0, index], recv_sem=sems.at[1, index],
            device_id=(peer,), device_id_type=MESH,
        )
        copy.start()
        return copy

    near_copies = [send(sums_ref, near.at[k], near_sems, k, near_peers[k - 1]) for k in range(1, GROUP)]
    width = HALO * SUP
    edges = [send(part_ref.at[:, pl.ds(rows * SUP, width)], left_buf, edge_sems, 0, right)]
    if both_ways:
        edges.append(send(part_ref.at[:, pl.ds(0, width)], right_buf, edge_sems, 1, left))
    for copy in near_copies:
        copy.wait()
    total = sums_ref[...]
    for k in range(1, GROUP):
        total = total + near[k]
    mine[...] = total
    far_copies = [send(mine, far.at[k], far_sems, k, far_peers[k - 1]) for k in range(1, groups)]
    for copy in far_copies:
        copy.wait()
    for k in range(1, groups):
        total = total + far[k]
    total_out[...] = total
    for copy in edges:
        copy.wait()
    left_out[...] = left_buf[...]
    if both_ways:
        right_out[...] = right_buf[...]


def exchange(part, sums, rows, both_ways, collective_id):
    edge = f32((FRAMES, HALO * SUP))
    edges = 2 if both_ways else 1
    groups = lax.axis_size("pts") // GROUP
    return pl.pallas_call(
        functools.partial(exchange_kernel, both_ways, rows),
        out_shape=(edge,) * edges + (f32((8, 128)),),
        in_specs=[VMEM, VMEM],
        out_specs=(VMEM,) * (edges + 1),
        scratch_shapes=[pltpu.VMEM(edge.shape, jnp.float32)] * edges
        + [
            pltpu.VMEM((GROUP, 8, 128), jnp.float32),
            pltpu.VMEM((groups, 8, 128), jnp.float32),
            pltpu.VMEM((8, 128), jnp.float32),
            pltpu.SemaphoreType.DMA((2, edges)),
            pltpu.SemaphoreType.DMA((2, GROUP)),
            pltpu.SemaphoreType.DMA((2, groups)),
        ],
        compiler_params=pltpu.CompilerParams(
            collective_id=collective_id, has_side_effects=True, vmem_limit_bytes=16 * 2**20
        ),
    )(part, sums)


def last_kernel(
    own_ref, image_ref, left_ref, part_ref, left2_ref, first_ref, second_ref, field_out, resid_out, field_ref, resid_ref, sems
):
    norm0, curve0 = frame_columns(first_ref[0:1])[:2]
    norm1, curve1, cross1 = frame_columns(second_ref[0:1])[:3]
    beta = norm1 / norm0
    alpha0 = wide(norm0 / curve0)
    alpha1 = wide(norm1 / (curve1 + 2.0 * beta * cross1 + beta * beta * curve0))
    beta = wide(beta)
    width = HALO * SUP
    copies = []
    for part in range(own_ref.shape[1] // width):
        def step(a, _):
            at = lanes(part * HALO + a)
            first, image, image_next = own_ref[:, at], image_ref[:, at], part_ref[:, at]
            if part == 0:
                image = image + left_ref[:, at]
                image_next = image_next + left2_ref[:, at]
            residual = first - alpha0 * image
            direction = residual + beta * first
            field_ref[:, at] = alpha0 * first + alpha1 * direction
            resid_ref[:, at] = residual - alpha1 * (image_next + beta * image)
            return 0

        loop(0, HALO, step, 0)
        at = pl.ds(part * width, width)
        for index, (src, dst) in enumerate(((field_ref, field_out), (resid_ref, resid_out))):
            copies.append(pltpu.make_async_copy(src.at[:, at], dst.at[:, at], sems.at[index, part]))
            copies[-1].start()
    for copy in copies:
        copy.wait()


def spans(positions, rows, limit):
    extent = positions.shape[1] // SUP
    boxed = positions.reshape(3, extent, SUP)
    low, high = jnp.min(boxed, axis=2), jnp.max(boxed, axis=2)
    index = jnp.arange(rows, dtype=jnp.int32)
    span = jnp.zeros((rows,), jnp.int32)
    for k in range(1, HALO + 1):
        ahead = slice(k, k + rows)
        gap = jnp.maximum(jnp.maximum(low[:, ahead] - high[:, :rows], low[:, :rows] - high[:, ahead]), 0.0)
        near = (jnp.sum(gap * gap, axis=0) < 1.0) & (index + k < limit)
        span = jnp.where(near, k, span)
    return jnp.concatenate([span, jnp.sum(span + 1, keepdims=True)])


def padded(positions):
    return UNIT * jnp.concatenate([positions, jnp.zeros((5, positions.shape[1]), jnp.float32)], axis=0)


def body(positions, noise, right_side, pairs, counts):
    rows = positions.shape[1] // SUP
    inner = rows - HALO
    width = HALO * SUP
    size = lax.axis_size("pts")
    back = [(i + 1, i) for i in range(size - 1)]
    edge_pos = lax.ppermute(positions[:, :width], "pts", back)
    halo = lax.ppermute(right_side[:, :width], "pts", back)
    noise = noise.reshape(1, -1)
    span = spans(positions, inner, rows)
    outer_pos = jnp.concatenate([positions[:, inner * SUP :], edge_pos], axis=1)
    outer_span = spans(outer_pos, HALO, jnp.where(lax.axis_index("pts") == size - 1, HALO, 2 * HALO))
    image, sums, keeps = first_pass(span, outer_span, positions, edge_pos, noise, right_side, halo)
    left, right, first = exchange(image, sums, rows, True, 0)
    part, sums = second_pass(span, outer_span, noise, right_side, halo, image, left, right, first, keeps)
    left2, second = exchange(part, sums, rows, False, 1)
    parts = rows // HALO
    return local_call(
        last_kernel, (right_side, image, left, part, left2, first, second),
        (f32(right_side.shape), f32(right_side.shape)),
        [pltpu.VMEM(right_side.shape, jnp.float32)] * 2 + [pltpu.SemaphoreType.DMA((2, parts))], 0, any_outs=2,
    )


def solution(mesh):
    in_specs = (P(None, "pts"), P("pts"), P(None, "pts"), P(None, "pts"), P("pts"))
    out_specs = (P(None, "pts"), P(None, "pts"))
    return jax.shard_map(body, mesh=mesh, in_specs=in_specs, out_specs=out_specs, check_vma=False)
```

```python
import functools

import jax
import jax.numpy as jnp
from jax import lax
from jax.experimental import pallas as pl
from jax.experimental.pallas import tpu as pltpu
from jax.sharding import PartitionSpec as P

SUP = 256
HALO = 8
FRAMES = 32
TINY = 1e-36
MESH = pl.DeviceIdType.MESH
VMEM = pl.BlockSpec(memory_space=pltpu.VMEM)
ANY = pl.BlockSpec(memory_space=pl.ANY)
SMEM = pl.BlockSpec(memory_space=pltpu.SMEM)
AHEAD = 3
BATCH = 8
EIGHT = jnp.float8_e4m3fn
UNIT = 8.0
KERNEL = UNIT**5 / 4
GROUP = 8


def f32(shape):
    return jax.ShapeDtypeStruct(shape, jnp.float32)


def dot(left, right, dim):
    return lax.dot_general(
        left, right, (((1,), (dim,)), ((), ())), preferred_element_type=jnp.float32
    )


def lanes(index, width=SUP):
    return pl.ds(pl.multiple_of(index * width, width), width)


def spread_rows(pos_ref, rows_ref, rows):
    row = lax.broadcasted_iota(jnp.int32, (32, 3 * 128), 0)
    lane = lax.broadcasted_iota(jnp.int32, (32, 3 * 128), 1)
    ones = ((row & 7) == (lane >> 7)).astype(jnp.float32).astype(jnp.bfloat16)

    def step(a, _):
        rest = pos_ref[:, lanes(a)]
        terms = []
        for _ in range(3):
            term = rest.astype(jnp.bfloat16).astype(jnp.float32)
            terms.append(term)
            rest = rest - term
        terms = jnp.concatenate(terms + [jnp.zeros_like(rest)], axis=0).astype(jnp.bfloat16)
        wide_rows = lax.dot_general(terms, ones, (((0,), (0,)), ((), ())), preferred_element_type=jnp.float32)
        for c in range(3):
            rows_ref[a, c] = wide_rows[:, c * 128 : (c + 1) * 128]
        return 0

    lax.fori_loop(0, rows, step, 0, unroll=4)


def scale_of(peak):
    peak = jnp.max(peak, axis=1, keepdims=True)
    return jnp.broadcast_to(224.0 / jnp.maximum(peak, 1e-30), (FRAMES, SUP))


def hold(vals_ref, a, values):
    high_ref, low_ref = vals_ref
    low_ref[a] = values.astype(EIGHT)
    high = values.astype(jnp.bfloat16)
    low = (values - high.astype(jnp.float32)).astype(jnp.bfloat16)
    high_ref[a] = jnp.concatenate([high, low], axis=0)


def follower(span_ref, rows):
    def following(a, c):
        last = c >= a + span_ref[0, a]
        a_next = jnp.minimum(jnp.where(last, a + 1, a), rows - 1)
        return a_next, jnp.where(last, a_next, c + 1)

    return following


def kernel_tile(pos_ref, rows_ref, a, c, high_ref, low_ref):
    highs, lows = [], []
    step = 32
    for i in range(0, SUP, step):
        pair = []
        for h in range(2):
            dist2 = None
            for axis in range(3):
                col = pos_ref[axis : axis + 1, pl.ds(pl.multiple_of(c * SUP + h * 128, 128), 128)]
                diff = rows_ref[a, axis, i : i + step, :] - col
                dist2 = diff * diff if axis == 0 else dist2 + diff * diff
            dist2 = jnp.maximum(dist2, TINY)
            reach = jnp.maximum(UNIT - dist2 * lax.rsqrt(dist2), 0.0)
            square = reach * reach
            kern = square * square * (1.25 * UNIT - reach)
            high = kern.astype(jnp.bfloat16)
            pair.append((high, (kern - high.astype(jnp.float32)).astype(EIGHT)))
        highs.append(jnp.concatenate([p[0] for p in pair], axis=1))
        lows.append(jnp.concatenate([p[1] for p in pair], axis=1))
        high_ref[i : i + step, :] = highs[-1]
        low_ref[i : i + step, :] = lows[-1]
    return jnp.concatenate(highs, axis=0), jnp.concatenate(lows, axis=0)


def products(vals_ref, out_ref, a, c, high, low, valid):
    high_ref, low_ref = vals_ref
    front = dot(high_ref[c], high, 1)
    front = front[:FRAMES] + front[FRAMES:] + dot(low_ref[c], low, 1)
    back = dot(high_ref[a], high, 0)
    back = back[:FRAMES] + back[FRAMES:] + dot(low_ref[a], low, 0)
    unused = out_ref.shape[1] // SUP - 1
    out_ref[:, lanes(jnp.where(valid, a, unused))] += front
    out_ref[:, lanes(jnp.where(valid & (a != c), c, unused))] += back


def group_count(total):
    return (total + BATCH - 1) // BATCH


def moves(tiles, keep, g, slots, save):
    slot = lax.rem(g, slots)
    stages, sems = tiles
    out = []
    for index in range(2):
        here, there = stages[index].at[slot], keep[index].at[g]
        src, dst = (here, there) if save else (there, here)
        out.append(pltpu.make_async_copy(src, dst, sems.at[index, slot]))
    return out


def sweep(span_ref, pos_ref, rows_ref, vals_ref, out_ref, rows, keep, tiles):
    total = span_ref[0, rows]
    groups = group_count(total)
    following = follower(span_ref, rows)
    highs, lows = tiles[0]

    def step(g, now):
        slot = lax.rem(g, 2)

        @pl.when(g >= 2)
        def _():
            for copy in moves(tiles, keep, g - 2, 2, True):
                copy.wait()

        for u in range(BATCH):
            a, c = now
            high, low = kernel_tile(pos_ref, rows_ref, a, c, highs.at[slot, u], lows.at[slot, u])
            products(vals_ref, out_ref, a, c, high, low, BATCH * g + u < total)
            now = following(a, c)
        for copy in moves(tiles, keep, g, 2, True):
            copy.start()
        return now

    lax.fori_loop(0, groups, step, (jnp.int32(0), jnp.int32(0)))
    for k in (2, 1):
        @pl.when(groups >= k)
        def _():
            for copy in moves(tiles, keep, groups - k, 2, True):
                copy.wait()


def fetch(keep, groups, tiles, g, begin):
    @pl.when(g < groups)
    def _():
        for copy in moves(tiles, keep, g, AHEAD + 1, False):
            if begin:
                copy.start()
            else:
                copy.wait()


def sweep_again(span_ref, rows, vals_ref, out_ref, keep, tiles):
    total = span_ref[0, rows]
    groups = group_count(total)
    following = follower(span_ref, rows)
    highs, lows = tiles[0]

    def step(g, now):
        slot = lax.rem(g, AHEAD + 1)
        fetch(keep, groups, tiles, g + AHEAD, True)
        fetch(keep, groups, tiles, g, False)
        for u in range(BATCH):
            a, c = now
            products(vals_ref, out_ref, a, c, highs[slot, u], lows[slot, u], BATCH * g + u < total)
            now = following(a, c)
        return now

    lax.fori_loop(0, groups, step, (jnp.int32(0), jnp.int32(0)))


def lane_totals(quantities):
    stacked = jnp.concatenate(quantities + [jnp.zeros_like(quantities[0])] * (4 - len(quantities)), axis=0)
    return jnp.broadcast_to(jnp.sum(jnp.transpose(stacked), axis=0, keepdims=True), (8, 128))


def frame_columns(totals):
    turned = jnp.transpose(jnp.broadcast_to(totals, (128, 128)))
    return [turned[i * FRAMES : (i + 1) * FRAMES] for i in range(4)]


def wide(column):
    return jnp.concatenate([column, column], axis=1)


def fold(values):
    return values[:, :128] + values[:, 128:]


def zeros():
    return jnp.zeros((FRAMES, 128), jnp.float32)


def loop(low, high, step, start):
    return lax.fori_loop(low, high, step, start, unroll=4)


def clear(out_ref, first, count):
    def step(a, _):
        out_ref[:, lanes(first + a)] = jnp.zeros((FRAMES, SUP), jnp.float32)
        return 0

    loop(0, count, step, 0)


def larger(peak, values):
    values = jnp.abs(values)
    return jnp.maximum(peak, jnp.maximum(values[:, :128], values[:, 128:]))


def first_kernel(
    span_ref, pos_ref, rows_ref, noise_ref, own_ref, halo_ref, out_ref, sums_ref, keep_high, keep_low, high_ref, low_ref, *stage
):
    rows = own_ref.shape[1] // SUP
    vals_ref, tiles = (high_ref, low_ref), (stage[:2], stage[2])
    peak = loop(0, rows, lambda a, peak: larger(peak, own_ref[:, lanes(a)]), zeros())
    scale = scale_of(loop(0, HALO, lambda a, peak: larger(peak, halo_ref[:, lanes(a)]), peak))
    clear(out_ref, 0, rows + HALO)

    def begin(a, norm):
        values = own_ref[:, lanes(a)]
        hold(vals_ref, a, scale * values)
        return norm + fold(values * values)

    def begin_halo(a, _):
        hold(vals_ref, rows + a, scale * halo_ref[:, lanes(a)])
        return 0

    norm = loop(0, rows, begin, zeros())
    loop(0, HALO, begin_halo, 0)
    sweep(span_ref, pos_ref, rows_ref, vals_ref, out_ref, rows, (keep_high, keep_low), tiles)
    inverse = 1.0 / (KERNEL * scale)

    def finish(a, curve):
        at = lanes(a)
        image = out_ref[:, at] * inverse + noise_ref[:, at] * own_ref[:, at]
        out_ref[:, at] = image
        return curve + fold(own_ref[:, at] * image)

    def finish_halo(a, curve):
        at = lanes(rows + a)
        image = out_ref[:, at] * inverse
        out_ref[:, at] = image
        return curve + fold(halo_ref[:, lanes(a)] * image)

    curve = loop(0, HALO, finish_halo, loop(0, rows, finish, zeros()))
    sums_ref[...] = lane_totals([norm, curve])


def second_kernel(
    span_ref, noise_ref, own_ref, halo_ref, image_ref, left_ref, right_ref, first_ref, keep_high, keep_low,
    out_ref, sums_ref, high_ref, low_ref, resid_ref, *stage
):
    vals_ref, tiles, keep = (high_ref, low_ref), (stage[:2], stage[2]), (keep_high, keep_low)
    rows = own_ref.shape[1] // SUP
    for g in range(AHEAD):
        fetch(keep, group_count(span_ref[0, rows]), tiles, g, True)
    norm_before, curve_before = frame_columns(first_ref[0:1])[:2]
    alpha = wide(norm_before / curve_before)

    def begin(a, image, values, sums):
        residual = values - alpha * image
        resid_ref[:, lanes(a)] = residual
        return (
            sums[0] + fold(residual * residual), sums[1] + fold(residual * image), larger(sums[2], residual)
        )

    def begin_first(a, sums):
        return begin(a, image_ref[:, lanes(a)] + left_ref[:, lanes(a)], own_ref[:, lanes(a)], sums)

    def begin_rest(a, sums):
        return begin(a, image_ref[:, lanes(a)], own_ref[:, lanes(a)], sums)

    sums = loop(0, HALO, begin_first, (zeros(), zeros(), zeros()))
    norm, cross, peak = loop(HALO, rows, begin_rest, sums)

    def begin_halo(a, peak):
        image = image_ref[:, lanes(rows + a)] + right_ref[:, lanes(a)]
        residual = halo_ref[:, lanes(a)] - alpha * image
        resid_ref[:, lanes(rows + a)] = residual
        return larger(peak, residual)

    scale = scale_of(loop(0, HALO, begin_halo, peak))

    def ready(a, _):
        hold(vals_ref, a, scale * resid_ref[:, lanes(a)])
        return 0

    loop(0, rows + HALO, ready, 0)
    clear(out_ref, 0, rows + HALO)
    sweep_again(span_ref, rows, vals_ref, out_ref, keep, tiles)
    inverse = 1.0 / (KERNEL * scale)

    def finish(a, curve):
        at = lanes(a)
        image = out_ref[:, at] * inverse + noise_ref[:, at] * resid_ref[:, at]
        out_ref[:, at] = image
        return curve + fold(resid_ref[:, at] * image)

    def finish_halo(a, curve):
        at = lanes(rows + a)
        image = out_ref[:, at] * inverse
        out_ref[:, at] = image
        return curve + fold(resid_ref[:, at] * image)

    curve = loop(0, HALO, finish_halo, loop(0, rows, finish, zeros()))
    sums_ref[...] = lane_totals([norm, curve, cross])


def vals_scratch(count):
    return [
        pltpu.VMEM((count, 2 * FRAMES, SUP), jnp.bfloat16),
        pltpu.VMEM((count, FRAMES, SUP), EIGHT),
    ]


def stage_scratch(slots):
    return [
        pltpu.VMEM((slots, BATCH, SUP, SUP), jnp.bfloat16),
        pltpu.VMEM((slots, BATCH, SUP, SUP), EIGHT),
        pltpu.SemaphoreType.DMA((2, slots)),
    ]


def kept(rows):
    steps = -(-rows * (HALO + 1) // BATCH)
    shape = (steps, BATCH, SUP, SUP)
    return jax.ShapeDtypeStruct(shape, jnp.bfloat16), jax.ShapeDtypeStruct(shape, EIGHT)


def first_pass(span, pos, spread, noise, right_side, halo):
    rows = right_side.shape[1] // SUP
    return local_call(
        first_kernel, (span, pos, spread, noise, right_side, halo),
        (f32((FRAMES, (rows + HALO + 1) * SUP)), f32((8, 128))) + kept(rows),
        vals_scratch(rows + HALO) + stage_scratch(2), 1, any_outs=2,
    )


def second_pass(span, noise, right_side, halo, image, left, right, first, keep):
    extent = right_side.shape[1] // SUP + HALO
    return local_call(
        second_kernel, (span, noise, right_side, halo, image, left, right, first, *keep),
        (f32((FRAMES, (extent + 1) * SUP)), f32((8, 128))),
        vals_scratch(extent) + [pltpu.VMEM((FRAMES, extent * SUP), jnp.float32)] + stage_scratch(AHEAD + 1), 1, anys=2, mib=50,
    )


def local_call(kernel, operands, out_shape, scratch, smalls, anys=0, any_outs=0, mib=28):
    plain = len(operands) - smalls - anys
    return pl.pallas_call(
        kernel,
        out_shape=out_shape,
        in_specs=[SMEM] * smalls + [VMEM] * plain + [ANY] * anys,
        out_specs=(VMEM,) * (len(out_shape) - any_outs) + (ANY,) * any_outs,
        scratch_shapes=scratch,
        compiler_params=pltpu.CompilerParams(vmem_limit_bytes=mib * 2**20),
    )(*operands)


def exchange_kernel(both_ways, rows, part_ref, sums_ref, *refs):
    if both_ways:
        left_out, right_out, total_out, left_buf, right_buf, near, far, mine, edge_sems, near_sems, far_sems = refs
    else:
        left_out, total_out, left_buf, near, far, mine, edge_sems, near_sems, far_sems = refs
    size = lax.axis_size("pts")
    me = lax.axis_index("pts")
    groups = size // GROUP
    spot, group = lax.rem(me, GROUP), me // GROUP
    right, left = lax.rem(me + 1, size), lax.rem(me + size - 1, size)
    near_peers = [group * GROUP + lax.rem(spot + k, GROUP) for k in range(1, GROUP)]
    far_peers = [lax.rem(group + k, groups) * GROUP + spot for k in range(1, groups)]
    barrier = pltpu.get_barrier_semaphore()
    peers = near_peers + far_peers + [left, right]
    for peer in peers:
        pl.semaphore_signal(barrier, inc=1, device_id=(peer,), device_id_type=MESH)
    pl.semaphore_wait(barrier, len(peers))

    def send(src, dst, sems, index, peer):
        copy = pltpu.make_async_remote_copy(
            src_ref=src, dst_ref=dst, send_sem=sems.at[0, index], recv_sem=sems.at[1, index],
            device_id=(peer,), device_id_type=MESH,
        )
        copy.start()
        return copy

    near_copies = [send(sums_ref, near.at[k], near_sems, k, near_peers[k - 1]) for k in range(1, GROUP)]
    width = HALO * SUP
    edges = [send(part_ref.at[:, pl.ds(rows * SUP, width)], left_buf, edge_sems, 0, right)]
    if both_ways:
        edges.append(send(part_ref.at[:, pl.ds(0, width)], right_buf, edge_sems, 1, left))
    for copy in near_copies:
        copy.wait()
    total = sums_ref[...]
    for k in range(1, GROUP):
        total = total + near[k]
    mine[...] = total
    far_copies = [send(mine, far.at[k], far_sems, k, far_peers[k - 1]) for k in range(1, groups)]
    for copy in far_copies:
        copy.wait()
    for k in range(1, groups):
        total = total + far[k]
    total_out[...] = total
    for copy in edges:
        copy.wait()
    left_out[...] = left_buf[...]
    if both_ways:
        right_out[...] = right_buf[...]


def exchange(part, sums, rows, both_ways, collective_id):
    edge = f32((FRAMES, HALO * SUP))
    edges = 2 if both_ways else 1
    groups = lax.axis_size("pts") // GROUP
    return pl.pallas_call(
        functools.partial(exchange_kernel, both_ways, rows),
        out_shape=(edge,) * edges + (f32((8, 128)),),
        in_specs=[VMEM, VMEM],
        out_specs=(VMEM,) * (edges + 1),
        scratch_shapes=[pltpu.VMEM(edge.shape, jnp.float32)] * edges
        + [
            pltpu.VMEM((GROUP, 8, 128), jnp.float32),
            pltpu.VMEM((groups, 8, 128), jnp.float32),
            pltpu.VMEM((8, 128), jnp.float32),
            pltpu.SemaphoreType.DMA((2, edges)),
            pltpu.SemaphoreType.DMA((2, GROUP)),
            pltpu.SemaphoreType.DMA((2, groups)),
        ],
        compiler_params=pltpu.CompilerParams(
            collective_id=collective_id, has_side_effects=True, vmem_limit_bytes=16 * 2**20
        ),
    )(part, sums)


def last_kernel(
    own_ref, image_ref, left_ref, part_ref, left2_ref, first_ref, second_ref, field_out, resid_out, field_ref, resid_ref, sems
):
    norm0, curve0 = frame_columns(first_ref[0:1])[:2]
    norm1, curve1, cross1 = frame_columns(second_ref[0:1])[:3]
    beta = norm1 / norm0
    alpha0 = wide(norm0 / curve0)
    alpha1 = wide(norm1 / (curve1 + 2.0 * beta * cross1 + beta * beta * curve0))
    beta = wide(beta)
    width = HALO * SUP
    copies = []
    for part in range(own_ref.shape[1] // width):
        def step(a, _):
            at = lanes(part * HALO + a)
            first, image, image_next = own_ref[:, at], image_ref[:, at], part_ref[:, at]
            if part == 0:
                image = image + left_ref[:, at]
                image_next = image_next + left2_ref[:, at]
            residual = first - alpha0 * image
            direction = residual + beta * first
            field_ref[:, at] = alpha0 * first + alpha1 * direction
            resid_ref[:, at] = residual - alpha1 * (image_next + beta * image)
            return 0

        loop(0, HALO, step, 0)
        at = pl.ds(part * width, width)
        for index, (src, dst) in enumerate(((field_ref, field_out), (resid_ref, resid_out))):
            copies.append(pltpu.make_async_copy(src.at[:, at], dst.at[:, at], sems.at[index, part]))
            copies[-1].start()
    for copy in copies:
        copy.wait()


def spans(boxes, rows, limit):
    low, high = boxes
    lane = lax.broadcasted_iota(jnp.int32, (1, 128), 1)
    span = jnp.zeros((1, 128), jnp.int32)
    for k in range(1, HALO + 1):
        low_k, high_k = pltpu.roll(low, 128 - k, 1), pltpu.roll(high, 128 - k, 1)
        gap = jnp.maximum(jnp.maximum(low_k - high, low - high_k), 0.0)
        near = (jnp.sum(gap * gap, axis=0, keepdims=True) < UNIT * UNIT) & (lane + k < limit)
        span = jnp.where(near, k, span)
    pairs = jnp.sum(jnp.where(lane < rows, span + 1, 0), axis=1, keepdims=True)
    return jnp.broadcast_to(jnp.where(lane == rows, pairs, span), (8, 128))


def start_kernel(positions_ref, own_ref, pos_ref, halo_ref, span_ref, rows_ref, edge_pos, edge, sems):
    rows = own_ref.shape[1] // SUP
    width = HALO * SUP
    size = lax.axis_size("pts")
    me = lax.axis_index("pts")
    right, left = lax.rem(me + 1, size), lax.rem(me + size - 1, size)
    barrier = pltpu.get_barrier_semaphore()
    for peer in (left, right):
        pl.semaphore_signal(barrier, inc=1, device_id=(peer,), device_id_type=MESH)
    blank = jnp.zeros((5, width), jnp.float32)
    for part in range(rows // HALO):
        at = slice(part * width, (part + 1) * width)
        pos_ref[:, at] = jnp.concatenate([UNIT * positions_ref[:, at], blank], axis=0)
    pl.semaphore_wait(barrier, 2)
    copies = []
    for index, (src, dst) in enumerate(((pos_ref, edge_pos), (own_ref, edge))):
        copies.append(
            pltpu.make_async_remote_copy(
                src_ref=src.at[:, pl.ds(0, width)], dst_ref=dst, send_sem=sems.at[0, index], recv_sem=sems.at[1, index],
                device_id=(left,), device_id_type=MESH,
            )
        )
        copies[-1].start()
    lane = lax.broadcasted_iota(jnp.int32, (8, 128), 1)

    def box(a, boxes):
        points = pos_ref[:, lanes(a)]
        low = jnp.min(jnp.minimum(points[:, :128], points[:, 128:]), axis=1, keepdims=True)
        high = jnp.max(jnp.maximum(points[:, :128], points[:, 128:]), axis=1, keepdims=True)
        return jnp.where(lane == a, low, boxes[0]), jnp.where(lane == a, high, boxes[1])

    none = jnp.zeros((8, 128), jnp.float32)
    boxes = loop(0, rows, box, (none, none))
    spread_rows(pos_ref, rows_ref, rows)
    for copy in copies:
        copy.wait()
    pos_ref[:, rows * SUP :] = edge_pos[...]
    halo_ref[...] = edge[...]
    boxes = loop(rows, rows + HALO, box, boxes)
    span_ref[...] = spans(boxes, rows, jnp.where(me == size - 1, rows, rows + HALO))


def start(positions, right_side, collective_id):
    rows = right_side.shape[1] // SUP
    width = HALO * SUP
    return pl.pallas_call(
        start_kernel,
        out_shape=(
            f32((8, (rows + HALO) * SUP)), f32((FRAMES, width)), jax.ShapeDtypeStruct((8, 128), jnp.int32),
            f32((rows, 3, SUP, 128)),
        ),
        in_specs=[VMEM, VMEM],
        out_specs=(VMEM,) * 4,
        scratch_shapes=[
            pltpu.VMEM((8, width), jnp.float32), pltpu.VMEM((FRAMES, width), jnp.float32), pltpu.SemaphoreType.DMA((2, 2)),
        ],
        compiler_params=pltpu.CompilerParams(
            collective_id=collective_id, has_side_effects=True, vmem_limit_bytes=28 * 2**20
        ),
    )(positions, right_side)


def body(positions, noise, right_side, pairs, counts):
    rows = positions.shape[1] // SUP
    noise = noise.reshape(1, -1)
    pos, halo, span, spread = start(positions, right_side, 2)
    image, sums, *keep = first_pass(span, pos, spread, noise, right_side, halo)
    left, right, first = exchange(image, sums, rows, True, 0)
    part, sums = second_pass(span, noise, right_side, halo, image, left, right, first, keep)
    left2, second = exchange(part, sums, rows, False, 1)
    parts = rows // HALO
    return local_call(
        last_kernel, (right_side, image, left, part, left2, first, second),
        (f32(right_side.shape), f32(right_side.shape)),
        [pltpu.VMEM(right_side.shape, jnp.float32)] * 2 + [pltpu.SemaphoreType.DMA((2, parts))], 0, any_outs=2,
    )


def solution(mesh):
    in_specs = (P(None, "pts"), P("pts"), P(None, "pts"), P(None, "pts"), P("pts"))
    out_specs = (P(None, "pts"), P(None, "pts"))
    return jax.shard_map(body, mesh=mesh, in_specs=in_specs, out_specs=out_specs, check_vma=False)
```

```python
import jax
import jax.numpy as jnp
from jax import lax
from jax.experimental import pallas as pl
from jax.experimental.pallas import tpu as pltpu
from jax.sharding import PartitionSpec as P

SUP = 256
HALO = 8
FRAMES = 32
TINY = 1e-36
MESH = pl.DeviceIdType.MESH
VMEM = pl.BlockSpec(memory_space=pltpu.VMEM)
ANY = pl.BlockSpec(memory_space=pl.ANY)
SMEM = pl.BlockSpec(memory_space=pltpu.SMEM)
AHEAD = 3
BATCH = 8
EIGHT = jnp.float8_e4m3fn
UNIT = 8.0
KERNEL = UNIT**5 / 4
GROUP = 8


def f32(shape):
    return jax.ShapeDtypeStruct(shape, jnp.float32)


def dot(left, right, dim):
    return lax.dot_general(
        left, right, (((1,), (dim,)), ((), ())), preferred_element_type=jnp.float32
    )


def lanes(index, width=SUP):
    return pl.ds(pl.multiple_of(index * width, width), width)


def spread_rows(pos_ref, rows_ref, rows):
    row = lax.broadcasted_iota(jnp.int32, (32, 3 * 128), 0)
    lane = lax.broadcasted_iota(jnp.int32, (32, 3 * 128), 1)
    ones = ((row & 7) == (lane >> 7)).astype(jnp.float32).astype(jnp.bfloat16)

    def step(a, _):
        rest = pos_ref[:, lanes(a)]
        terms = []
        for _ in range(3):
            term = rest.astype(jnp.bfloat16).astype(jnp.float32)
            terms.append(term)
            rest = rest - term
        terms = jnp.concatenate(terms + [jnp.zeros_like(rest)], axis=0).astype(jnp.bfloat16)
        wide_rows = lax.dot_general(terms, ones, (((0,), (0,)), ((), ())), preferred_element_type=jnp.float32)
        for c in range(3):
            rows_ref[a, c] = wide_rows[:, c * 128 : (c + 1) * 128]
        return 0

    lax.fori_loop(0, rows, step, 0, unroll=4)


def scale_of(peak):
    peak = jnp.max(peak, axis=1, keepdims=True)
    return jnp.broadcast_to(224.0 / jnp.maximum(peak, 1e-30), (FRAMES, SUP))


def hold(vals_ref, a, values):
    high_ref, low_ref = vals_ref
    low_ref[a] = values.astype(EIGHT)
    high = values.astype(jnp.bfloat16)
    low = (values - high.astype(jnp.float32)).astype(jnp.bfloat16)
    high_ref[a] = jnp.concatenate([high, low], axis=0)


def follower(span_ref, rows):
    def following(a, c):
        last = c >= a + span_ref[0, a]
        a_next = jnp.minimum(jnp.where(last, a + 1, a), rows - 1)
        return a_next, jnp.where(last, a_next, c + 1)

    return following


def kernel_tile(pos_ref, rows_ref, a, c, high_ref, low_ref):
    highs, lows = [], []
    step = 32
    for i in range(0, SUP, step):
        pair = []
        for h in range(2):
            dist2 = None
            for axis in range(3):
                col = pos_ref[axis : axis + 1, pl.ds(pl.multiple_of(c * SUP + h * 128, 128), 128)]
                diff = rows_ref[a, axis, i : i + step, :] - col
                dist2 = diff * diff if axis == 0 else dist2 + diff * diff
            dist2 = jnp.maximum(dist2, TINY)
            reach = jnp.maximum(UNIT - dist2 * lax.rsqrt(dist2), 0.0)
            square = reach * reach
            kern = square * square * (1.25 * UNIT - reach)
            high = kern.astype(jnp.bfloat16)
            pair.append((high, (kern - high.astype(jnp.float32)).astype(EIGHT)))
        highs.append(jnp.concatenate([p[0] for p in pair], axis=1))
        lows.append(jnp.concatenate([p[1] for p in pair], axis=1))
        high_ref[i : i + step, :] = highs[-1]
        low_ref[i : i + step, :] = lows[-1]
    return jnp.concatenate(highs, axis=0), jnp.concatenate(lows, axis=0)


def products(vals_ref, out_ref, a, c, high, low, valid):
    high_ref, low_ref = vals_ref
    front = dot(high_ref[c], high, 1)
    front = front[:FRAMES] + front[FRAMES:] + dot(low_ref[c], low, 1)
    back = dot(high_ref[a], high, 0)
    back = back[:FRAMES] + back[FRAMES:] + dot(low_ref[a], low, 0)
    unused = out_ref.shape[1] // SUP - 1
    out_ref[:, lanes(jnp.where(valid, a, unused))] += front
    out_ref[:, lanes(jnp.where(valid & (a != c), c, unused))] += back


def group_count(total):
    return (total + BATCH - 1) // BATCH


def moves(tiles, keep, g, slots, save):
    slot = lax.rem(g, slots)
    stages, sems = tiles
    out = []
    for index in range(2):
        here, there = stages[index].at[slot], keep[index].at[g]
        src, dst = (here, there) if save else (there, here)
        out.append(pltpu.make_async_copy(src, dst, sems.at[index, slot]))
    return out


def sweep(span_ref, pos_ref, rows_ref, vals_ref, out_ref, rows, keep, tiles):
    total = span_ref[0, rows]
    groups = group_count(total)
    following = follower(span_ref, rows)
    highs, lows = tiles[0]

    def step(g, now):
        slot = lax.rem(g, 2)

        @pl.when(g >= 2)
        def _():
            for copy in moves(tiles, keep, g - 2, 2, True):
                copy.wait()

        for u in range(BATCH):
            a, c = now
            high, low = kernel_tile(pos_ref, rows_ref, a, c, highs.at[slot, u], lows.at[slot, u])
            products(vals_ref, out_ref, a, c, high, low, BATCH * g + u < total)
            now = following(a, c)
        for copy in moves(tiles, keep, g, 2, True):
            copy.start()
        return now

    lax.fori_loop(0, groups, step, (jnp.int32(0), jnp.int32(0)))


def settle(span_ref, rows, keep, tiles):
    groups = group_count(span_ref[0, rows])
    for k in (2, 1):
        @pl.when(groups >= k)
        def _():
            for copy in moves(tiles, keep, groups - k, 2, True):
                copy.wait()


def fetch(keep, groups, tiles, g, begin):
    @pl.when(g < groups)
    def _():
        for copy in moves(tiles, keep, g, AHEAD + 1, False):
            if begin:
                copy.start()
            else:
                copy.wait()


def sweep_again(span_ref, rows, vals_ref, out_ref, keep, tiles):
    total = span_ref[0, rows]
    groups = group_count(total)
    following = follower(span_ref, rows)
    highs, lows = tiles[0]

    def step(g, now):
        slot = lax.rem(g, AHEAD + 1)
        fetch(keep, groups, tiles, g + AHEAD, True)
        fetch(keep, groups, tiles, g, False)
        for u in range(BATCH):
            a, c = now
            products(vals_ref, out_ref, a, c, highs[slot, u], lows[slot, u], BATCH * g + u < total)
            now = following(a, c)
        return now

    lax.fori_loop(0, groups, step, (jnp.int32(0), jnp.int32(0)))


def lane_totals(quantities):
    stacked = jnp.concatenate(quantities + [jnp.zeros_like(quantities[0])] * (4 - len(quantities)), axis=0)
    return jnp.broadcast_to(jnp.sum(jnp.transpose(stacked), axis=0, keepdims=True), (8, 128))


def frame_columns(totals):
    turned = jnp.transpose(jnp.broadcast_to(totals, (128, 128)))
    return [turned[i * FRAMES : (i + 1) * FRAMES] for i in range(4)]


def wide(column):
    return jnp.concatenate([column, column], axis=1)


def fold(values):
    return values[:, :128] + values[:, 128:]


def zeros():
    return jnp.zeros((FRAMES, 128), jnp.float32)


def loop(low, high, step, start):
    return lax.fori_loop(low, high, step, start, unroll=4)


def clear(out_ref, first, count):
    def step(a, _):
        out_ref[:, lanes(first + a)] = jnp.zeros((FRAMES, SUP), jnp.float32)
        return 0

    loop(0, count, step, 0)


def larger(peak, values):
    values = jnp.abs(values)
    return jnp.maximum(peak, jnp.maximum(values[:, :128], values[:, 128:]))


def first_kernel(
    span_ref, pos_ref, rows_ref, noise_ref, own_ref, halo_ref, out_ref, sums_ref, keep_high, keep_low, high_ref, low_ref, *stage
):
    rows = own_ref.shape[1] // SUP
    vals_ref, tiles = (high_ref, low_ref), (stage[:2], stage[2])
    peak = loop(0, rows, lambda a, peak: larger(peak, own_ref[:, lanes(a)]), zeros())
    scale = scale_of(loop(0, HALO, lambda a, peak: larger(peak, halo_ref[:, lanes(a)]), peak))
    clear(out_ref, 0, rows + HALO)

    def begin(a, norm):
        values = own_ref[:, lanes(a)]
        hold(vals_ref, a, scale * values)
        return norm + fold(values * values)

    def begin_halo(a, _):
        hold(vals_ref, rows + a, scale * halo_ref[:, lanes(a)])
        return 0

    norm = loop(0, rows, begin, zeros())
    loop(0, HALO, begin_halo, 0)
    sweep(span_ref, pos_ref, rows_ref, vals_ref, out_ref, rows, (keep_high, keep_low), tiles)
    inverse = 1.0 / (KERNEL * scale)

    def finish(a, curve):
        at = lanes(a)
        image = out_ref[:, at] * inverse + noise_ref[:, at] * own_ref[:, at]
        out_ref[:, at] = image
        return curve + fold(own_ref[:, at] * image)

    def finish_halo(a, curve):
        at = lanes(rows + a)
        image = out_ref[:, at] * inverse
        out_ref[:, at] = image
        return curve + fold(halo_ref[:, lanes(a)] * image)

    curve = loop(0, HALO, finish_halo, loop(0, rows, finish, zeros()))
    sums_ref[...] = lane_totals([norm, curve])
    settle(span_ref, rows, (keep_high, keep_low), tiles)


def second_kernel(
    span_ref, noise_ref, own_ref, halo_ref, image_ref, left_ref, right_ref, first_ref, keep_high, keep_low,
    out_ref, resid_ref, inverse_ref, sums_ref, high_ref, low_ref, *stage
):
    vals_ref, tiles, keep = (high_ref, low_ref), (stage[:2], stage[2]), (keep_high, keep_low)
    rows = own_ref.shape[1] // SUP
    for g in range(AHEAD):
        fetch(keep, group_count(span_ref[0, rows]), tiles, g, True)
    norm_before, curve_before = frame_columns(first_ref[0:1])[:2]
    alpha = wide(norm_before / curve_before)

    def begin(a, image, values, sums):
        residual = values - alpha * image
        resid_ref[:, lanes(a)] = residual
        return (
            sums[0] + fold(residual * residual), sums[1] + fold(residual * image), larger(sums[2], residual)
        )

    def begin_first(a, sums):
        return begin(a, image_ref[:, lanes(a)] + left_ref[:, lanes(a)], own_ref[:, lanes(a)], sums)

    def begin_rest(a, sums):
        return begin(a, image_ref[:, lanes(a)], own_ref[:, lanes(a)], sums)

    sums = loop(0, HALO, begin_first, (zeros(), zeros(), zeros()))
    norm, cross, peak = loop(HALO, rows, begin_rest, sums)

    def begin_halo(a, peak):
        image = image_ref[:, lanes(rows + a)] + right_ref[:, lanes(a)]
        residual = halo_ref[:, lanes(a)] - alpha * image
        resid_ref[:, lanes(rows + a)] = residual
        return larger(peak, residual)

    scale = scale_of(loop(0, HALO, begin_halo, peak))

    def ready(a, _):
        hold(vals_ref, a, scale * resid_ref[:, lanes(a)])
        return 0

    loop(0, rows + HALO, ready, 0)
    clear(out_ref, 0, rows + HALO)
    sweep_again(span_ref, rows, vals_ref, out_ref, keep, tiles)
    inverse_ref[...] = 1.0 / (KERNEL * scale)
    sums_ref[0], sums_ref[1] = norm, cross


def vals_scratch(count):
    return [
        pltpu.VMEM((count, 2 * FRAMES, SUP), jnp.bfloat16),
        pltpu.VMEM((count, FRAMES, SUP), EIGHT),
    ]


def stage_scratch(slots):
    return [
        pltpu.VMEM((slots, BATCH, SUP, SUP), jnp.bfloat16),
        pltpu.VMEM((slots, BATCH, SUP, SUP), EIGHT),
        pltpu.SemaphoreType.DMA((2, slots)),
    ]


def kept(rows):
    steps = -(-rows * (HALO + 1) // BATCH)
    shape = (steps, BATCH, SUP, SUP)
    return jax.ShapeDtypeStruct(shape, jnp.bfloat16), jax.ShapeDtypeStruct(shape, EIGHT)


def first_pass(span, pos, spread, noise, right_side, halo):
    rows = right_side.shape[1] // SUP
    return local_call(
        first_kernel, (span, pos, spread, noise, right_side, halo),
        (f32((FRAMES, (rows + HALO + 1) * SUP)), f32((8, 128))) + kept(rows),
        vals_scratch(rows + HALO) + stage_scratch(2), 1, any_outs=2,
    )


def second_pass(span, noise, right_side, halo, image, left, right, first, keep):
    extent = right_side.shape[1] // SUP + HALO
    return local_call(
        second_kernel, (span, noise, right_side, halo, image, left, right, first, *keep),
        (f32((FRAMES, (extent + 1) * SUP)), f32((FRAMES, extent * SUP)), f32((FRAMES, SUP)), f32((2, FRAMES, 128))),
        vals_scratch(extent) + stage_scratch(AHEAD + 1), 1, anys=2, mib=44,
    )


def local_call(kernel, operands, out_shape, scratch, smalls, anys=0, any_outs=0, mib=28):
    plain = len(operands) - smalls - anys
    return pl.pallas_call(
        kernel,
        out_shape=out_shape,
        in_specs=[SMEM] * smalls + [VMEM] * plain + [ANY] * anys,
        out_specs=(VMEM,) * (len(out_shape) - any_outs) + (ANY,) * any_outs,
        scratch_shapes=scratch,
        compiler_params=pltpu.CompilerParams(vmem_limit_bytes=mib * 2**20),
    )(*operands)


def arrive(peers):
    barrier = pltpu.get_barrier_semaphore()
    for peer in peers:
        pl.semaphore_signal(barrier, inc=1, device_id=(peer,), device_id_type=MESH)
    return lambda: pl.semaphore_wait(barrier, len(peers))


def send(src, dst, sems, index, peer):
    copy = pltpu.make_async_remote_copy(
        src_ref=src, dst_ref=dst, send_sem=sems.at[0, index], recv_sem=sems.at[1, index],
        device_id=(peer,), device_id_type=MESH,
    )
    copy.start()
    return copy


def neighbours():
    size, me = lax.axis_size("pts"), lax.axis_index("pts")
    return lax.rem(me + size - 1, size), lax.rem(me + 1, size)


def partners():
    me = lax.axis_index("pts")
    groups = lax.axis_size("pts") // GROUP
    spot, group = lax.rem(me, GROUP), me // GROUP
    near_peers = [group * GROUP + lax.rem(spot + k, GROUP) for k in range(1, GROUP)]
    far_peers = [lax.rem(group + k, groups) * GROUP + spot for k in range(1, groups)]
    return near_peers, far_peers


def sum_over_devices(total, mine, slots, sems, edges):
    offset = 0
    for stage, peers in enumerate(partners()):
        mine[stage, 0:1] = total
        copies = [
            send(mine.at[stage, pl.ds(0, 1)], slots.at[offset + k, pl.ds(0, 1)], sems, offset + k, peer)
            for k, peer in enumerate(peers)
        ]
        if stage == 0:
            edges()
        for copy in copies:
            copy.wait()
        for k in range(len(peers)):
            total = total + slots[offset + k, 0:1]
        offset += len(peers)
    return total


def exchange_kernel(
    part_ref, sums_ref, left_out, right_out, total_out, left_buf, right_buf, slots, mine, edge_sems, sems
):
    near_peers, far_peers = partners()
    left, right = neighbours()
    arrive(near_peers + far_peers + [left, right])()
    width = left_buf.shape[1]
    first = part_ref.shape[1] - width - SUP
    copies = []

    def edges():
        copies.append(send(part_ref.at[:, pl.ds(first, width)], left_buf, edge_sems, 0, right))
        copies.append(send(part_ref.at[:, pl.ds(0, width)], right_buf, edge_sems, 1, left))

    total = sum_over_devices(sums_ref[0:1], mine, slots, sems, edges)
    total_out[...] = jnp.broadcast_to(total, (8, 128))
    for copy in copies:
        copy.wait()
    left_out[...] = left_buf[...]
    right_out[...] = right_buf[...]


def finish_kernel(
    part_ref, resid_ref, inverse_ref, norms_ref, noise_ref, image_out, left_out, total_out,
    edge, left_buf, slots, mine, edge_sems, sems
):
    near_peers, far_peers = partners()
    left, right = neighbours()
    arrived = arrive(near_peers + far_peers + [left, right])
    rows = image_out.shape[1] // SUP
    inverse = inverse_ref[...]

    def finish(a, curve):
        at = lanes(a)
        image = part_ref[:, at] * inverse + noise_ref[:, at] * resid_ref[:, at]
        image_out[:, at] = image
        return curve + fold(resid_ref[:, at] * image)

    def finish_halo(a, curve):
        at = lanes(rows + a)
        image = part_ref[:, at] * inverse
        edge[:, lanes(a)] = image
        return curve + fold(resid_ref[:, at] * image)

    curve = loop(0, HALO, finish_halo, loop(0, rows, finish, zeros()))
    total = lane_totals([norms_ref[0], curve, norms_ref[1]])[0:1]
    arrived()
    copies = []
    total = sum_over_devices(
        total, mine, slots, sems, lambda: copies.append(send(edge, left_buf, edge_sems, 0, right))
    )
    total_out[...] = jnp.broadcast_to(total, (8, 128))
    for copy in copies:
        copy.wait()
    left_out[...] = left_buf[...]


def remote_call(kernel, operands, out_shape, scratch, collective_id):
    partners_count = GROUP - 1 + lax.axis_size("pts") // GROUP - 1
    return pl.pallas_call(
        kernel,
        out_shape=out_shape,
        in_specs=[VMEM] * len(operands),
        out_specs=(VMEM,) * len(out_shape),
        scratch_shapes=scratch
        + [
            pltpu.VMEM((partners_count, 8, 128), jnp.float32),
            pltpu.VMEM((2, 8, 128), jnp.float32),
            pltpu.SemaphoreType.DMA((2, 2)),
            pltpu.SemaphoreType.DMA((2, partners_count)),
        ],
        compiler_params=pltpu.CompilerParams(
            collective_id=collective_id, has_side_effects=True, vmem_limit_bytes=16 * 2**20
        ),
    )(*operands)


def last_kernel(
    own_ref, image_ref, left_ref, part_ref, left2_ref, first_ref, second_ref, field_out, resid_out, field_ref, resid_ref, sems
):
    norm0, curve0 = frame_columns(first_ref[0:1])[:2]
    norm1, curve1, cross1 = frame_columns(second_ref[0:1])[:3]
    beta = norm1 / norm0
    alpha0 = wide(norm0 / curve0)
    alpha1 = wide(norm1 / (curve1 + 2.0 * beta * cross1 + beta * beta * curve0))
    beta = wide(beta)
    width = HALO * SUP
    copies = []
    for part in range(own_ref.shape[1] // width):
        def step(a, _):
            at = lanes(part * HALO + a)
            first, image, image_next = own_ref[:, at], image_ref[:, at], part_ref[:, at]
            if part == 0:
                image = image + left_ref[:, at]
                image_next = image_next + left2_ref[:, at]
            residual = first - alpha0 * image
            direction = residual + beta * first
            field_ref[:, at] = alpha0 * first + alpha1 * direction
            resid_ref[:, at] = residual - alpha1 * (image_next + beta * image)
            return 0

        loop(0, HALO, step, 0)
        at = pl.ds(part * width, width)
        for index, (src, dst) in enumerate(((field_ref, field_out), (resid_ref, resid_out))):
            copies.append(pltpu.make_async_copy(src.at[:, at], dst.at[:, at], sems.at[index, part]))
            copies[-1].start()
    for copy in copies:
        copy.wait()


def spans(boxes, rows, limit):
    low, high = boxes
    lane = lax.broadcasted_iota(jnp.int32, (1, 128), 1)
    span = jnp.zeros((1, 128), jnp.int32)
    for k in range(1, HALO + 1):
        low_k, high_k = pltpu.roll(low, 128 - k, 1), pltpu.roll(high, 128 - k, 1)
        gap = jnp.maximum(jnp.maximum(low_k - high, low - high_k), 0.0)
        near = (jnp.sum(gap * gap, axis=0, keepdims=True) < UNIT * UNIT) & (lane + k < limit)
        span = jnp.where(near, k, span)
    pairs = jnp.sum(jnp.where(lane < rows, span + 1, 0), axis=1, keepdims=True)
    return jnp.broadcast_to(jnp.where(lane == rows, pairs, span), (8, 128))


def start_kernel(
    positions_any, own_any, pos_ref, halo_ref, span_ref, rows_ref, own_out, positions_ref, edge_pos, edge, local_sems, sems
):
    rows = own_any.shape[1] // SUP
    width = HALO * SUP
    size = lax.axis_size("pts")
    me = lax.axis_index("pts")
    right, left = lax.rem(me + 1, size), lax.rem(me + size - 1, size)
    barrier = pltpu.get_barrier_semaphore()
    for peer in (left, right):
        pl.semaphore_signal(barrier, inc=1, device_id=(peer,), device_id_type=MESH)
    bring = pltpu.make_async_copy(positions_any, positions_ref, local_sems.at[0])
    bring.start()
    pass_on = pltpu.make_async_copy(own_any, own_out, local_sems.at[1])
    pass_on.start()
    pl.semaphore_wait(barrier, 2)
    copies = []
    for index, (src, dst) in enumerate(((positions_any, edge_pos), (own_any, edge))):
        copies.append(
            pltpu.make_async_remote_copy(
                src_ref=src.at[:, pl.ds(0, width)], dst_ref=dst, send_sem=sems.at[0, index], recv_sem=sems.at[1, index],
                device_id=(left,), device_id_type=MESH,
            )
        )
        copies[-1].start()
    bring.wait()
    blank = jnp.zeros((5, width), jnp.float32)
    for part in range(rows // HALO):
        at = slice(part * width, (part + 1) * width)
        pos_ref[:, at] = jnp.concatenate([UNIT * positions_ref[:, at], blank], axis=0)
    lane = lax.broadcasted_iota(jnp.int32, (8, 128), 1)

    def box(a, boxes):
        points = pos_ref[:, lanes(a)]
        low = jnp.min(jnp.minimum(points[:, :128], points[:, 128:]), axis=1, keepdims=True)
        high = jnp.max(jnp.maximum(points[:, :128], points[:, 128:]), axis=1, keepdims=True)
        return jnp.where(lane == a, low, boxes[0]), jnp.where(lane == a, high, boxes[1])

    none = jnp.zeros((8, 128), jnp.float32)
    boxes = loop(0, rows, box, (none, none))
    spread_rows(pos_ref, rows_ref, rows)
    for copy in copies:
        copy.wait()
    pass_on.wait()
    pos_ref[:, rows * SUP :] = jnp.concatenate([UNIT * edge_pos[...], blank], axis=0)
    halo_ref[...] = edge[...]
    boxes = loop(rows, rows + HALO, box, boxes)
    span_ref[...] = spans(boxes, rows, jnp.where(me == size - 1, rows, rows + HALO))


def start(positions, right_side, collective_id):
    rows = right_side.shape[1] // SUP
    width = HALO * SUP
    return pl.pallas_call(
        start_kernel,
        out_shape=(
            f32((8, (rows + HALO) * SUP)), f32((FRAMES, width)), jax.ShapeDtypeStruct((8, 128), jnp.int32),
            f32((rows, 3, SUP, 128)), f32(right_side.shape),
        ),
        in_specs=[ANY, VMEM],
        out_specs=(VMEM,) * 5,
        scratch_shapes=[
            pltpu.VMEM(positions.shape, jnp.float32),
            pltpu.VMEM((3, width), jnp.float32),
            pltpu.VMEM((FRAMES, width), jnp.float32),
            pltpu.SemaphoreType.DMA((2,)),
            pltpu.SemaphoreType.DMA((2, 2)),
        ],
        compiler_params=pltpu.CompilerParams(
            collective_id=collective_id, has_side_effects=True, vmem_limit_bytes=28 * 2**20
        ),
    )(positions, right_side)


def body(positions, noise, right_side, pairs, counts):
    rows = positions.shape[1] // SUP
    noise = noise.reshape(1, -1)
    pos, halo, span, spread, right_side = start(positions, right_side, 2)
    image, sums, *keep = first_pass(span, pos, spread, noise, right_side, halo)
    edge = f32(halo.shape)
    held = pltpu.VMEM(halo.shape, jnp.float32)
    left, right, first = remote_call(exchange_kernel, (image, sums), (edge, edge, f32((8, 128))), [held] * 2, 0)
    part, resid, inverse, norms = second_pass(span, noise, right_side, halo, image, left, right, first, keep)
    part, left2, second = remote_call(
        finish_kernel, (part, resid, inverse, norms, noise), (f32(right_side.shape), edge, f32((8, 128))), [held] * 2, 1
    )
    parts = rows // HALO
    return local_call(
        last_kernel, (right_side, image, left, part, left2, first, second),
        (f32(right_side.shape), f32(right_side.shape)),
        [pltpu.VMEM(right_side.shape, jnp.float32)] * 2 + [pltpu.SemaphoreType.DMA((2, parts))], 0, any_outs=2,
    )


def solution(mesh):
    in_specs = (P(None, "pts"), P("pts"), P(None, "pts"), P(None, "pts"), P("pts"))
    out_specs = (P(None, "pts"), P(None, "pts"))
    return jax.shard_map(body, mesh=mesh, in_specs=in_specs, out_specs=out_specs, check_vma=False)
```

```python
import jax
import jax.numpy as jnp
from jax import lax
from jax.experimental import pallas as pl
from jax.experimental.pallas import tpu as pltpu
from jax.sharding import PartitionSpec as P

SUP = 256
HALO = 8
FRAMES = 32
TINY = 1e-36
MESH = pl.DeviceIdType.MESH
VMEM = pl.BlockSpec(memory_space=pltpu.VMEM)
ANY = pl.BlockSpec(memory_space=pl.ANY)
SMEM = pl.BlockSpec(memory_space=pltpu.SMEM)
AHEAD = 3
BATCH = 16
EIGHT = jnp.float8_e4m3fn
UNIT = 8.0
KERNEL = UNIT**5 / 4
GROUP = 8


def f32(shape):
    return jax.ShapeDtypeStruct(shape, jnp.float32)


def dot(left, right, dim):
    return lax.dot_general(
        left, right, (((1,), (dim,)), ((), ())), preferred_element_type=jnp.float32
    )


def lanes(index, width=SUP):
    return pl.ds(pl.multiple_of(index * width, width), width)


def spread_rows(pos_ref, rows_ref, rows):
    row = lax.broadcasted_iota(jnp.int32, (32, 3 * 128), 0)
    lane = lax.broadcasted_iota(jnp.int32, (32, 3 * 128), 1)
    ones = ((row & 7) == (lane >> 7)).astype(jnp.float32).astype(jnp.bfloat16)

    def step(a, _):
        rest = pos_ref[:, lanes(a)]
        terms = []
        for _ in range(3):
            term = rest.astype(jnp.bfloat16).astype(jnp.float32)
            terms.append(term)
            rest = rest - term
        terms = jnp.concatenate(terms + [jnp.zeros_like(rest)], axis=0).astype(jnp.bfloat16)
        wide_rows = lax.dot_general(terms, ones, (((0,), (0,)), ((), ())), preferred_element_type=jnp.float32)
        for c in range(3):
            rows_ref[a, c] = wide_rows[:, c * 128 : (c + 1) * 128]
        return 0

    lax.fori_loop(0, rows, step, 0, unroll=4)


def scale_of(peak):
    peak = jnp.max(peak, axis=1, keepdims=True)
    return jnp.broadcast_to(224.0 / jnp.maximum(peak, 1e-30), (FRAMES, SUP))


def hold(vals_ref, a, values):
    high_ref, low_ref = vals_ref
    low_ref[a] = values.astype(EIGHT)
    high = values.astype(jnp.bfloat16)
    low = (values - high.astype(jnp.float32)).astype(jnp.bfloat16)
    high_ref[a] = jnp.concatenate([high, low], axis=0)


def follower(span_ref, rows):
    def following(a, c):
        last = c >= a + span_ref[0, a]
        a_next = jnp.minimum(jnp.where(last, a + 1, a), rows - 1)
        return a_next, jnp.where(last, a_next, c + 1)

    return following


def kernel_tile(pos_ref, rows_ref, a, c, high_ref, low_ref):
    highs, lows = [], []
    step = 32
    for i in range(0, SUP, step):
        pair = []
        for h in range(2):
            dist2 = None
            for axis in range(3):
                col = pos_ref[axis : axis + 1, pl.ds(pl.multiple_of(c * SUP + h * 128, 128), 128)]
                diff = rows_ref[a, axis, i : i + step, :] - col
                dist2 = diff * diff if axis == 0 else dist2 + diff * diff
            dist2 = jnp.maximum(dist2, TINY)
            reach = jnp.maximum(UNIT - dist2 * lax.rsqrt(dist2), 0.0)
            square = reach * reach
            kern = square * square * (1.25 * UNIT - reach)
            high = kern.astype(jnp.bfloat16)
            pair.append((high, (kern - high.astype(jnp.float32)).astype(EIGHT)))
        highs.append(jnp.concatenate([p[0] for p in pair], axis=1))
        lows.append(jnp.concatenate([p[1] for p in pair], axis=1))
        high_ref[i : i + step, :] = highs[-1]
        low_ref[i : i + step, :] = lows[-1]
    return jnp.concatenate(highs, axis=0), jnp.concatenate(lows, axis=0)


def products(vals_ref, out_ref, a, c, high, low, valid):
    high_ref, low_ref = vals_ref
    front = dot(high_ref[c], high, 1)
    front = front[:FRAMES] + front[FRAMES:] + dot(low_ref[c], low, 1)
    back = dot(high_ref[a], high, 0)
    back = back[:FRAMES] + back[FRAMES:] + dot(low_ref[a], low, 0)
    unused = out_ref.shape[1] // SUP - 1
    out_ref[:, lanes(jnp.where(valid, a, unused))] += front
    out_ref[:, lanes(jnp.where(valid & (a != c), c, unused))] += back


def group_count(total):
    return (total + BATCH - 1) // BATCH


def moves(tiles, keep, g, slots, save):
    slot = lax.rem(g, slots)
    stages, sems = tiles
    out = []
    for index in range(2):
        here, there = stages[index].at[slot], keep[index].at[g]
        src, dst = (here, there) if save else (there, here)
        out.append(pltpu.make_async_copy(src, dst, sems.at[index, slot]))
    return out


def sweep(span_ref, pos_ref, rows_ref, vals_ref, out_ref, rows, keep, tiles):
    total = span_ref[0, rows]
    groups = group_count(total)
    following = follower(span_ref, rows)
    highs, lows = tiles[0]

    def step(g, now):
        slot = lax.rem(g, 2)

        @pl.when(g >= 2)
        def _():
            for copy in moves(tiles, keep, g - 2, 2, True):
                copy.wait()

        for u in range(BATCH):
            a, c = now
            high, low = kernel_tile(pos_ref, rows_ref, a, c, highs.at[slot, u], lows.at[slot, u])
            products(vals_ref, out_ref, a, c, highs[slot, u], lows[slot, u], BATCH * g + u < total)
            now = following(a, c)
        for copy in moves(tiles, keep, g, 2, True):
            copy.start()
        return now

    lax.fori_loop(0, groups, step, (jnp.int32(0), jnp.int32(0)))


def settle(span_ref, rows, keep, tiles):
    groups = group_count(span_ref[0, rows])
    for k in (2, 1):
        @pl.when(groups >= k)
        def _():
            for copy in moves(tiles, keep, groups - k, 2, True):
                copy.wait()


def fetch(keep, groups, tiles, g, begin):
    @pl.when(g < groups)
    def _():
        for copy in moves(tiles, keep, g, AHEAD + 1, False):
            if begin:
                copy.start()
            else:
                copy.wait()


def sweep_again(span_ref, rows, vals_ref, out_ref, keep, tiles):
    total = span_ref[0, rows]
    groups = group_count(total)
    following = follower(span_ref, rows)
    highs, lows = tiles[0]

    def step(g, now):
        slot = lax.rem(g, AHEAD + 1)
        fetch(keep, groups, tiles, g + AHEAD, True)
        fetch(keep, groups, tiles, g, False)
        for u in range(BATCH):
            a, c = now
            products(vals_ref, out_ref, a, c, highs[slot, u], lows[slot, u], BATCH * g + u < total)
            now = following(a, c)
        return now

    lax.fori_loop(0, groups, step, (jnp.int32(0), jnp.int32(0)))


def lane_totals(quantities):
    stacked = jnp.concatenate(quantities + [jnp.zeros_like(quantities[0])] * (4 - len(quantities)), axis=0)
    return jnp.broadcast_to(jnp.sum(jnp.transpose(stacked), axis=0, keepdims=True), (8, 128))


def frame_columns(totals):
    turned = jnp.transpose(jnp.broadcast_to(totals, (128, 128)))
    return [turned[i * FRAMES : (i + 1) * FRAMES] for i in range(4)]


def wide(column):
    return jnp.concatenate([column, column], axis=1)


def fold(values):
    return values[:, :128] + values[:, 128:]


def zeros():
    return jnp.zeros((FRAMES, 128), jnp.float32)


def loop(low, high, step, start):
    return lax.fori_loop(low, high, step, start, unroll=4)


def clear(out_ref, first, count):
    def step(a, _):
        out_ref[:, lanes(first + a)] = jnp.zeros((FRAMES, SUP), jnp.float32)
        return 0

    loop(0, count, step, 0)


def larger(peak, values):
    values = jnp.abs(values)
    return jnp.maximum(peak, jnp.maximum(values[:, :128], values[:, 128:]))


def first_kernel(
    span_ref, pos_ref, rows_ref, noise_ref, own_ref, halo_ref, out_ref, sums_ref, keep_high, keep_low, high_ref, low_ref, *stage
):
    rows = own_ref.shape[1] // SUP
    vals_ref, tiles = (high_ref, low_ref), (stage[:2], stage[2])
    peak = loop(0, rows, lambda a, peak: larger(peak, own_ref[:, lanes(a)]), zeros())
    scale = scale_of(loop(0, HALO, lambda a, peak: larger(peak, halo_ref[:, lanes(a)]), peak))
    clear(out_ref, 0, rows + HALO)

    def begin(a, norm):
        values = own_ref[:, lanes(a)]
        hold(vals_ref, a, scale * values)
        return norm + fold(values * values)

    def begin_halo(a, _):
        hold(vals_ref, rows + a, scale * halo_ref[:, lanes(a)])
        return 0

    norm = loop(0, rows, begin, zeros())
    loop(0, HALO, begin_halo, 0)
    sweep(span_ref, pos_ref, rows_ref, vals_ref, out_ref, rows, (keep_high, keep_low), tiles)
    inverse = 1.0 / (KERNEL * scale)

    def finish(a, curve):
        at = lanes(a)
        image = out_ref[:, at] * inverse + noise_ref[:, at] * own_ref[:, at]
        out_ref[:, at] = image
        return curve + fold(own_ref[:, at] * image)

    def finish_halo(a, curve):
        at = lanes(rows + a)
        image = out_ref[:, at] * inverse
        out_ref[:, at] = image
        return curve + fold(halo_ref[:, lanes(a)] * image)

    curve = loop(0, HALO, finish_halo, loop(0, rows, finish, zeros()))
    sums_ref[...] = lane_totals([norm, curve])
    settle(span_ref, rows, (keep_high, keep_low), tiles)


def second_kernel(
    span_ref, noise_ref, own_ref, halo_ref, image_ref, left_ref, right_ref, first_ref, keep_high, keep_low,
    out_ref, resid_ref, inverse_ref, sums_ref, high_ref, low_ref, *stage
):
    vals_ref, tiles, keep = (high_ref, low_ref), (stage[:2], stage[2]), (keep_high, keep_low)
    rows = own_ref.shape[1] // SUP
    for g in range(AHEAD):
        fetch(keep, group_count(span_ref[0, rows]), tiles, g, True)
    norm_before, curve_before = frame_columns(first_ref[0:1])[:2]
    alpha = wide(norm_before / curve_before)

    def begin(a, image, values, sums):
        residual = values - alpha * image
        resid_ref[:, lanes(a)] = residual
        return (
            sums[0] + fold(residual * residual), sums[1] + fold(residual * image), larger(sums[2], residual)
        )

    def begin_first(a, sums):
        return begin(a, image_ref[:, lanes(a)] + left_ref[:, lanes(a)], own_ref[:, lanes(a)], sums)

    def begin_rest(a, sums):
        return begin(a, image_ref[:, lanes(a)], own_ref[:, lanes(a)], sums)

    sums = loop(0, HALO, begin_first, (zeros(), zeros(), zeros()))
    norm, cross, peak = loop(HALO, rows, begin_rest, sums)

    def begin_halo(a, peak):
        image = image_ref[:, lanes(rows + a)] + right_ref[:, lanes(a)]
        residual = halo_ref[:, lanes(a)] - alpha * image
        resid_ref[:, lanes(rows + a)] = residual
        return larger(peak, residual)

    scale = scale_of(loop(0, HALO, begin_halo, peak))

    def ready(a, _):
        hold(vals_ref, a, scale * resid_ref[:, lanes(a)])
        return 0

    loop(0, rows + HALO, ready, 0)
    clear(out_ref, 0, rows + HALO)
    sweep_again(span_ref, rows, vals_ref, out_ref, keep, tiles)
    inverse_ref[...] = 1.0 / (KERNEL * scale)
    sums_ref[0], sums_ref[1] = norm, cross


def vals_scratch(count):
    return [
        pltpu.VMEM((count, 2 * FRAMES, SUP), jnp.bfloat16),
        pltpu.VMEM((count, FRAMES, SUP), EIGHT),
    ]


def stage_scratch(slots):
    return [
        pltpu.VMEM((slots, BATCH, SUP, SUP), jnp.bfloat16),
        pltpu.VMEM((slots, BATCH, SUP, SUP), EIGHT),
        pltpu.SemaphoreType.DMA((2, slots)),
    ]


def kept(rows):
    steps = -(-rows * (HALO + 1) // BATCH)
    shape = (steps, BATCH, SUP, SUP)
    return jax.ShapeDtypeStruct(shape, jnp.bfloat16), jax.ShapeDtypeStruct(shape, EIGHT)


def first_pass(span, pos, spread, noise, right_side, halo):
    rows = right_side.shape[1] // SUP
    return local_call(
        first_kernel, (span, pos, spread, noise, right_side, halo),
        (f32((FRAMES, (rows + HALO + 1) * SUP)), f32((8, 128))) + kept(rows),
        vals_scratch(rows + HALO) + stage_scratch(2), 1, any_outs=2,
    )


def second_pass(span, noise, right_side, halo, image, left, right, first, keep):
    extent = right_side.shape[1] // SUP + HALO
    return local_call(
        second_kernel, (span, noise, right_side, halo, image, left, right, first, *keep),
        (f32((FRAMES, (extent + 1) * SUP)), f32((FRAMES, extent * SUP)), f32((FRAMES, SUP)), f32((2, FRAMES, 128))),
        vals_scratch(extent) + stage_scratch(AHEAD + 1), 1, anys=2, mib=44,
    )


def local_call(kernel, operands, out_shape, scratch, smalls, anys=0, any_outs=0, mib=32):
    plain = len(operands) - smalls - anys
    return pl.pallas_call(
        kernel,
        out_shape=out_shape,
        in_specs=[SMEM] * smalls + [VMEM] * plain + [ANY] * anys,
        out_specs=(VMEM,) * (len(out_shape) - any_outs) + (ANY,) * any_outs,
        scratch_shapes=scratch,
        compiler_params=pltpu.CompilerParams(vmem_limit_bytes=mib * 2**20),
    )(*operands)


def arrive(peers):
    barrier = pltpu.get_barrier_semaphore()
    for peer in peers:
        pl.semaphore_signal(barrier, inc=1, device_id=(peer,), device_id_type=MESH)
    return lambda: pl.semaphore_wait(barrier, len(peers))


def send(src, dst, sems, index, peer):
    copy = pltpu.make_async_remote_copy(
        src_ref=src, dst_ref=dst, send_sem=sems.at[0, index], recv_sem=sems.at[1, index],
        device_id=(peer,), device_id_type=MESH,
    )
    copy.start()
    return copy


def neighbours():
    size, me = lax.axis_size("pts"), lax.axis_index("pts")
    return lax.rem(me + size - 1, size), lax.rem(me + 1, size)


def partners():
    me = lax.axis_index("pts")
    groups = lax.axis_size("pts") // GROUP
    spot, group = lax.rem(me, GROUP), me // GROUP
    near_peers = [group * GROUP + lax.rem(spot + k, GROUP) for k in range(1, GROUP)]
    far_peers = [lax.rem(group + k, groups) * GROUP + spot for k in range(1, groups)]
    return near_peers, far_peers


def sum_over_devices(total, mine, slots, sems, edges):
    for stage, peers in enumerate(partners()):
        mine[stage, 0:1] = total
        for k, peer in enumerate(peers):
            pltpu.make_async_remote_copy(
                src_ref=mine.at[stage, pl.ds(0, 1)], dst_ref=slots.at[stage, pl.ds(k, 1)],
                send_sem=sems.at[0, stage], recv_sem=sems.at[1, stage], device_id=(peer,), device_id_type=MESH,
            ).start()
        if stage == 0:
            edges()
        rows = slots.at[stage, pl.ds(0, len(peers))]
        for side in range(2):
            pltpu.make_async_copy(rows, rows, sems.at[side, stage]).wait()
        total = total + jnp.sum(slots[stage, 0 : len(peers)], axis=0, keepdims=True)
    return total


def exchange_kernel(
    part_ref, sums_ref, left_out, right_out, total_out, left_buf, right_buf, slots, mine, edge_sems, sems
):
    near_peers, far_peers = partners()
    left, right = neighbours()
    arrive(near_peers + far_peers + [left, right])()
    width = left_buf.shape[1]
    first = part_ref.shape[1] - width - SUP
    copies = []

    def edges():
        copies.append(send(part_ref.at[:, pl.ds(first, width)], left_buf, edge_sems, 0, right))
        copies.append(send(part_ref.at[:, pl.ds(0, width)], right_buf, edge_sems, 1, left))

    total = sum_over_devices(sums_ref[0:1], mine, slots, sems, edges)
    total_out[...] = jnp.broadcast_to(total, (8, 128))
    for copy in copies:
        copy.wait()
    left_out[...] = left_buf[...]
    right_out[...] = right_buf[...]


def finish_kernel(
    part_ref, resid_ref, inverse_ref, norms_ref, noise_ref, image_out, left_out, total_out,
    edge, left_buf, slots, mine, edge_sems, sems
):
    near_peers, far_peers = partners()
    left, right = neighbours()
    arrived = arrive(near_peers + far_peers + [left, right])
    rows = image_out.shape[1] // SUP
    inverse = inverse_ref[...]

    def finish(a, curve):
        at = lanes(a)
        image = part_ref[:, at] * inverse + noise_ref[:, at] * resid_ref[:, at]
        image_out[:, at] = image
        return curve + fold(resid_ref[:, at] * image)

    def finish_halo(a, curve):
        at = lanes(rows + a)
        image = part_ref[:, at] * inverse
        edge[:, lanes(a)] = image
        return curve + fold(resid_ref[:, at] * image)

    curve = loop(0, HALO, finish_halo, loop(0, rows, finish, zeros()))
    total = lane_totals([norms_ref[0], curve, norms_ref[1]])[0:1]
    arrived()
    copies = []
    total = sum_over_devices(
        total, mine, slots, sems, lambda: copies.append(send(edge, left_buf, edge_sems, 0, right))
    )
    total_out[...] = jnp.broadcast_to(total, (8, 128))
    for copy in copies:
        copy.wait()
    left_out[...] = left_buf[...]


def remote_call(kernel, operands, out_shape, scratch, collective_id):
    most = -(-lax.axis_size("pts") // GROUP // 8) * 8
    return pl.pallas_call(
        kernel,
        out_shape=out_shape,
        in_specs=[VMEM] * len(operands),
        out_specs=(VMEM,) * len(out_shape),
        scratch_shapes=scratch
        + [
            pltpu.VMEM((2, most, 128), jnp.float32),
            pltpu.VMEM((2, 8, 128), jnp.float32),
            pltpu.SemaphoreType.DMA((2, 2)),
            pltpu.SemaphoreType.DMA((2, 2)),
        ],
        compiler_params=pltpu.CompilerParams(
            collective_id=collective_id, has_side_effects=True, vmem_limit_bytes=16 * 2**20
        ),
    )(*operands)


def last_kernel(
    own_ref, image_ref, left_ref, part_ref, left2_ref, first_ref, second_ref, field_out, resid_out, field_ref, resid_ref, sems
):
    norm0, curve0 = frame_columns(first_ref[0:1])[:2]
    norm1, curve1, cross1 = frame_columns(second_ref[0:1])[:3]
    beta = norm1 / norm0
    alpha0 = wide(norm0 / curve0)
    alpha1 = wide(norm1 / (curve1 + 2.0 * beta * cross1 + beta * beta * curve0))
    beta = wide(beta)
    width = HALO * SUP
    copies = []
    for part in range(own_ref.shape[1] // width):
        def step(a, _):
            at = lanes(part * HALO + a)
            first, image, image_next = own_ref[:, at], image_ref[:, at], part_ref[:, at]
            if part == 0:
                image = image + left_ref[:, at]
                image_next = image_next + left2_ref[:, at]
            residual = first - alpha0 * image
            direction = residual + beta * first
            field_ref[:, at] = alpha0 * first + alpha1 * direction
            resid_ref[:, at] = residual - alpha1 * (image_next + beta * image)
            return 0

        loop(0, HALO, step, 0)
        at = pl.ds(part * width, width)
        for index, (src, dst) in enumerate(((field_ref, field_out), (resid_ref, resid_out))):
            copies.append(pltpu.make_async_copy(src.at[:, at], dst.at[:, at], sems.at[index, part]))
            copies[-1].start()
    for copy in copies:
        copy.wait()


def spans(boxes, rows, limit):
    low, high = boxes
    lane = lax.broadcasted_iota(jnp.int32, (1, 128), 1)
    span = jnp.zeros((1, 128), jnp.int32)
    for k in range(1, HALO + 1):
        low_k, high_k = pltpu.roll(low, 128 - k, 1), pltpu.roll(high, 128 - k, 1)
        gap = jnp.maximum(jnp.maximum(low_k - high, low - high_k), 0.0)
        near = (jnp.sum(gap * gap, axis=0, keepdims=True) < UNIT * UNIT) & (lane + k < limit)
        span = jnp.where(near, k, span)
    pairs = jnp.sum(jnp.where(lane < rows, span + 1, 0), axis=1, keepdims=True)
    return jnp.broadcast_to(jnp.where(lane == rows, pairs, span), (8, 128))


def start_kernel(
    positions_any, own_any, pos_ref, halo_ref, span_ref, rows_ref, own_out, positions_ref, edge_pos, edge, local_sems, sems
):
    rows = own_any.shape[1] // SUP
    width = HALO * SUP
    size = lax.axis_size("pts")
    me = lax.axis_index("pts")
    right, left = lax.rem(me + 1, size), lax.rem(me + size - 1, size)
    barrier = pltpu.get_barrier_semaphore()
    for peer in (left, right):
        pl.semaphore_signal(barrier, inc=1, device_id=(peer,), device_id_type=MESH)
    bring = pltpu.make_async_copy(positions_any, positions_ref, local_sems.at[0])
    bring.start()
    pass_on = pltpu.make_async_copy(own_any, own_out, local_sems.at[1])
    pass_on.start()
    pl.semaphore_wait(barrier, 2)
    copies = []
    for index, (src, dst) in enumerate(((positions_any, edge_pos), (own_any, edge))):
        copies.append(
            pltpu.make_async_remote_copy(
                src_ref=src.at[:, pl.ds(0, width)], dst_ref=dst, send_sem=sems.at[0, index], recv_sem=sems.at[1, index],
                device_id=(left,), device_id_type=MESH,
            )
        )
        copies[-1].start()
    bring.wait()
    blank = jnp.zeros((5, width), jnp.float32)
    for part in range(rows // HALO):
        at = slice(part * width, (part + 1) * width)
        pos_ref[:, at] = jnp.concatenate([UNIT * positions_ref[:, at], blank], axis=0)
    lane = lax.broadcasted_iota(jnp.int32, (8, 128), 1)

    def box(a, boxes):
        points = pos_ref[:, lanes(a)]
        low = jnp.min(jnp.minimum(points[:, :128], points[:, 128:]), axis=1, keepdims=True)
        high = jnp.max(jnp.maximum(points[:, :128], points[:, 128:]), axis=1, keepdims=True)
        return jnp.where(lane == a, low, boxes[0]), jnp.where(lane == a, high, boxes[1])

    none = jnp.zeros((8, 128), jnp.float32)
    boxes = loop(0, rows, box, (none, none))
    spread_rows(pos_ref, rows_ref, rows)
    for copy in copies:
        copy.wait()
    pass_on.wait()
    pos_ref[:, rows * SUP :] = jnp.concatenate([UNIT * edge_pos[...], blank], axis=0)
    halo_ref[...] = edge[...]
    boxes = loop(rows, rows + HALO, box, boxes)
    span_ref[...] = spans(boxes, rows, jnp.where(me == size - 1, rows, rows + HALO))


def start(positions, right_side, collective_id):
    rows = right_side.shape[1] // SUP
    width = HALO * SUP
    return pl.pallas_call(
        start_kernel,
        out_shape=(
            f32((8, (rows + HALO) * SUP)), f32((FRAMES, width)), jax.ShapeDtypeStruct((8, 128), jnp.int32),
            f32((rows, 3, SUP, 128)), f32(right_side.shape),
        ),
        in_specs=[ANY, VMEM],
        out_specs=(VMEM,) * 5,
        scratch_shapes=[
            pltpu.VMEM(positions.shape, jnp.float32),
            pltpu.VMEM((3, width), jnp.float32),
            pltpu.VMEM((FRAMES, width), jnp.float32),
            pltpu.SemaphoreType.DMA((2,)),
            pltpu.SemaphoreType.DMA((2, 2)),
        ],
        compiler_params=pltpu.CompilerParams(
            collective_id=collective_id, has_side_effects=True, vmem_limit_bytes=28 * 2**20
        ),
    )(positions, right_side)


def body(positions, noise, right_side, pairs, counts):
    rows = positions.shape[1] // SUP
    noise = noise.reshape(1, -1)
    pos, halo, span, spread, right_side = start(positions, right_side, 2)
    image, sums, *keep = first_pass(span, pos, spread, noise, right_side, halo)
    edge = f32(halo.shape)
    held = pltpu.VMEM(halo.shape, jnp.float32)
    left, right, first = remote_call(exchange_kernel, (image, sums), (edge, edge, f32((8, 128))), [held] * 2, 0)
    part, resid, inverse, norms = second_pass(span, noise, right_side, halo, image, left, right, first, keep)
    part, left2, second = remote_call(
        finish_kernel, (part, resid, inverse, norms, noise), (f32(right_side.shape), edge, f32((8, 128))), [held] * 2, 1
    )
    parts = rows // HALO
    return local_call(
        last_kernel, (right_side, image, left, part, left2, first, second),
        (f32(right_side.shape), f32(right_side.shape)),
        [pltpu.VMEM(right_side.shape, jnp.float32)] * 2 + [pltpu.SemaphoreType.DMA((2, parts))], 0, any_outs=2,
    )


def solution(mesh):
    in_specs = (P(None, "pts"), P("pts"), P(None, "pts"), P(None, "pts"), P("pts"))
    out_specs = (P(None, "pts"), P(None, "pts"))
    return jax.shard_map(body, mesh=mesh, in_specs=in_specs, out_specs=out_specs, check_vma=False)
```

```python
import jax
import jax.numpy as jnp
from jax import lax
from jax.experimental import pallas as pl
from jax.experimental.pallas import tpu as pltpu
from jax.sharding import PartitionSpec as P

SUP = 256
HALO = 8
FRAMES = 32
TINY = 1e-36
MESH = pl.DeviceIdType.MESH
VMEM = pl.BlockSpec(memory_space=pltpu.VMEM)
ANY = pl.BlockSpec(memory_space=pl.ANY)
SMEM = pl.BlockSpec(memory_space=pltpu.SMEM)
AHEAD = 3
BATCH = 16
EIGHT = jnp.float8_e4m3fn
UNIT = 8.0
KERNEL = UNIT**5 / 4
GROUP = 8


def f32(shape):
    return jax.ShapeDtypeStruct(shape, jnp.float32)


def dot(left, right, dim):
    return lax.dot_general(
        left, right, (((1,), (dim,)), ((), ())), preferred_element_type=jnp.float32
    )


def lanes(index, width=SUP):
    return pl.ds(pl.multiple_of(index * width, width), width)


def spread_rows(pos_ref, rows_ref, rows):
    row = lax.broadcasted_iota(jnp.int32, (32, 3 * 128), 0)
    lane = lax.broadcasted_iota(jnp.int32, (32, 3 * 128), 1)
    ones = ((row & 7) == (lane >> 7)).astype(jnp.float32).astype(jnp.bfloat16)

    def step(a, _):
        rest = pos_ref[:, lanes(a)]
        terms = []
        for _ in range(3):
            term = rest.astype(jnp.bfloat16).astype(jnp.float32)
            terms.append(term)
            rest = rest - term
        terms = jnp.concatenate(terms + [jnp.zeros_like(rest)], axis=0).astype(jnp.bfloat16)
        wide_rows = lax.dot_general(terms, ones, (((0,), (0,)), ((), ())), preferred_element_type=jnp.float32)
        for c in range(3):
            rows_ref[a, c] = wide_rows[:, c * 128 : (c + 1) * 128]
        return 0

    lax.fori_loop(0, rows, step, 0, unroll=4)


def scale_of(peak):
    peak = jnp.max(peak, axis=1, keepdims=True)
    return jnp.broadcast_to(224.0 / jnp.maximum(peak, 1e-30), (FRAMES, SUP))


def hold(vals_ref, a, values):
    high_ref, low_ref = vals_ref
    low_ref[a] = values.astype(EIGHT)
    high = values.astype(jnp.bfloat16)
    low = (values - high.astype(jnp.float32)).astype(jnp.bfloat16)
    high_ref[a] = jnp.concatenate([high, low], axis=0)


def visited(span_ref, a, before):
    return (span_ref[0, a] > 0) | jnp.logical_not(before)


def pair_count(span_ref, rows):
    def step(a, carry):
        count, before = carry
        here = visited(span_ref, a, before)
        return count + jnp.where(here, jnp.maximum(span_ref[0, a], 1), 0), here

    return lax.fori_loop(0, rows, step, (jnp.int32(0), True))[0]


def first_pair(span_ref):
    a = jnp.where(span_ref[0, 0] > 0, 0, 1)
    return a, a + 1


def following(span_ref, rows, a, c):
    last = c >= a + span_ref[0, a]
    after = jnp.minimum(jnp.where(span_ref[0, a + 1] > 0, a + 1, a + 2), rows - 1)
    a_next = jnp.where(last, after, a)
    return a_next, jnp.where(last, after, c) + 1


def kernel_part(pos_ref, rows_ref, a, c, i, step, h):
    dist2 = None
    for axis in range(3):
        col = pos_ref[axis : axis + 1, pl.ds(pl.multiple_of(c * SUP + h * 128, 128), 128)]
        diff = rows_ref[a, axis, i : i + step, :] - col
        dist2 = diff * diff if axis == 0 else dist2 + diff * diff
    dist2 = jnp.maximum(dist2, TINY)
    reach = jnp.maximum(UNIT - dist2 * lax.rsqrt(dist2), 0.0)
    square = reach * reach
    return square * square * (1.25 * UNIT - reach)


def put(tile, i, step, kerns):
    highs = [kern.astype(jnp.bfloat16) for kern in kerns]
    lows = [(kern - high.astype(jnp.float32)).astype(EIGHT) for kern, high in zip(kerns, highs)]
    tile[0][i : i + step, :] = jnp.concatenate(highs, axis=1)
    tile[1][i : i + step, :] = jnp.concatenate(lows, axis=1)


def pair_tile(pos_ref, rows_ref, a, c, tile):
    for i in range(0, SUP, 32):
        put(tile, i, 32, [kernel_part(pos_ref, rows_ref, a, c, i, 32, h) for h in range(2)])


def own_tile(pos_ref, rows_ref, a, tile):
    quarter = []
    for i in range(0, 128, 32):
        quarter.append(kernel_part(pos_ref, rows_ref, a, a, i, 32, 1))
        put(tile, i, 32, [kernel_part(pos_ref, rows_ref, a, a, i, 32, 0), quarter[-1]])
    turned = jnp.transpose(jnp.concatenate(quarter, axis=0))
    for i in range(0, 128, 32):
        put(tile, 128 + i, 32, [turned[i : i + 32], kernel_part(pos_ref, rows_ref, a, a, 128 + i, 32, 1)])


def product(vals_ref, a, tile, dim):
    high_ref, low_ref = vals_ref
    both = dot(high_ref[a], tile[0][...], dim)
    return both[:FRAMES] + both[FRAMES:] + dot(low_ref[a], tile[1][...], dim)


def pair_products(vals_ref, out_ref, a, c, tile, valid):
    front, back = product(vals_ref, c, tile, 1), product(vals_ref, a, tile, 0)
    unused = out_ref.shape[1] // SUP - 1
    out_ref[:, lanes(jnp.where(valid, a, unused))] += front
    out_ref[:, lanes(jnp.where(valid, c, unused))] += back


def own_products(vals_ref, out_ref, a, tile):
    out_ref[:, lanes(a)] += product(vals_ref, a, tile, 0)


def group_count(span_ref, rows):
    return rows // BATCH + (pair_count(span_ref, rows) + BATCH - 1) // BATCH


def moves(tiles, keep, g, slots, save):
    slot = lax.rem(g, slots)
    stages, sems = tiles
    out = []
    for index in range(2):
        here, there = stages[index].at[slot], keep[index].at[g]
        src, dst = (here, there) if save else (there, here)
        out.append(pltpu.make_async_copy(src, dst, sems.at[index, slot]))
    return out


def each_tile(span_ref, rows, tiles, slots, groups, begin, own, pair, end):
    highs, lows = tiles[0]
    count = pair_count(span_ref, rows)

    def tile(g, u):
        slot = lax.rem(g, slots)
        return highs.at[slot, u], lows.at[slot, u]

    def own_step(g, _):
        begin(g)
        for u in range(BATCH):
            own(g * BATCH + u, tile(g, u))
        end(g)
        return 0

    lax.fori_loop(0, rows // BATCH, own_step, 0)

    def pair_step(g, now):
        begin(g)
        for u in range(BATCH):
            a, c = now
            valid = ((g - rows // BATCH) * BATCH + u < count) & (c <= a + span_ref[0, a])
            pair(a, c, tile(g, u), valid)
            now = following(span_ref, rows, a, c)
        end(g)
        return now

    lax.fori_loop(rows // BATCH, groups, pair_step, first_pair(span_ref))


def sweep(span_ref, pos_ref, rows_ref, vals_ref, out_ref, rows, keep, tiles):
    def begin(g):
        @pl.when(g >= 2)
        def _():
            for copy in moves(tiles, keep, g - 2, 2, True):
                copy.wait()

    def end(g):
        for copy in moves(tiles, keep, g, 2, True):
            copy.start()

    def own(a, tile):
        own_tile(pos_ref, rows_ref, a, tile)
        own_products(vals_ref, out_ref, a, tile)

    def pair(a, c, tile, valid):
        pair_tile(pos_ref, rows_ref, a, c, tile)
        pair_products(vals_ref, out_ref, a, c, tile, valid)

    each_tile(span_ref, rows, tiles, 2, group_count(span_ref, rows), begin, own, pair, end)


def settle(span_ref, rows, keep, tiles):
    groups = group_count(span_ref, rows)
    for k in (2, 1):
        @pl.when(groups >= k)
        def _():
            for copy in moves(tiles, keep, groups - k, 2, True):
                copy.wait()


def fetch(keep, groups, tiles, g, begin):
    @pl.when(g < groups)
    def _():
        for copy in moves(tiles, keep, g, AHEAD + 1, False):
            if begin:
                copy.start()
            else:
                copy.wait()


def sweep_again(span_ref, rows, groups, vals_ref, out_ref, keep, tiles):
    def begin(g):
        fetch(keep, groups, tiles, g + AHEAD, True)
        fetch(keep, groups, tiles, g, False)

    def own(a, tile):
        own_products(vals_ref, out_ref, a, tile)

    def pair(a, c, tile, valid):
        pair_products(vals_ref, out_ref, a, c, tile, valid)

    each_tile(span_ref, rows, tiles, AHEAD + 1, groups, begin, own, pair, lambda g: None)


def lane_totals(quantities):
    stacked = jnp.concatenate(quantities + [jnp.zeros_like(quantities[0])] * (4 - len(quantities)), axis=0)
    return jnp.broadcast_to(jnp.sum(jnp.transpose(stacked), axis=0, keepdims=True), (8, 128))


def frame_columns(totals):
    turned = jnp.transpose(jnp.broadcast_to(totals, (128, 128)))
    return [turned[i * FRAMES : (i + 1) * FRAMES] for i in range(4)]


def wide(column):
    return jnp.concatenate([column, column], axis=1)


def fold(values):
    return values[:, :128] + values[:, 128:]


def zeros():
    return jnp.zeros((FRAMES, 128), jnp.float32)


def loop(low, high, step, start):
    return lax.fori_loop(low, high, step, start, unroll=4)


def clear(out_ref, first, count):
    def step(a, _):
        out_ref[:, lanes(first + a)] = jnp.zeros((FRAMES, SUP), jnp.float32)
        return 0

    loop(0, count, step, 0)


def larger(peak, values):
    values = jnp.abs(values)
    return jnp.maximum(peak, jnp.maximum(values[:, :128], values[:, 128:]))


def first_kernel(
    span_ref, pos_ref, rows_ref, noise_ref, own_ref, halo_ref, out_ref, sums_ref, keep_high, keep_low, high_ref, low_ref, *stage
):
    rows = own_ref.shape[1] // SUP
    vals_ref, tiles = (high_ref, low_ref), (stage[:2], stage[2])
    peak = loop(0, rows, lambda a, peak: larger(peak, own_ref[:, lanes(a)]), zeros())
    scale = scale_of(loop(0, HALO, lambda a, peak: larger(peak, halo_ref[:, lanes(a)]), peak))
    clear(out_ref, 0, rows + HALO)

    def begin(a, norm):
        values = own_ref[:, lanes(a)]
        hold(vals_ref, a, scale * values)
        return norm + fold(values * values)

    def begin_halo(a, _):
        hold(vals_ref, rows + a, scale * halo_ref[:, lanes(a)])
        return 0

    norm = loop(0, rows, begin, zeros())
    loop(0, HALO, begin_halo, 0)
    sweep(span_ref, pos_ref, rows_ref, vals_ref, out_ref, rows, (keep_high, keep_low), tiles)
    inverse = 1.0 / (KERNEL * scale)

    def finish(a, curve):
        at = lanes(a)
        image = out_ref[:, at] * inverse + noise_ref[:, at] * own_ref[:, at]
        out_ref[:, at] = image
        return curve + fold(own_ref[:, at] * image)

    def finish_halo(a, curve):
        at = lanes(rows + a)
        image = out_ref[:, at] * inverse
        out_ref[:, at] = image
        return curve + fold(halo_ref[:, lanes(a)] * image)

    curve = loop(0, HALO, finish_halo, loop(0, rows, finish, zeros()))
    sums_ref[...] = lane_totals([norm, curve])
    settle(span_ref, rows, (keep_high, keep_low), tiles)


def second_kernel(
    span_ref, noise_ref, own_ref, halo_ref, image_ref, left_ref, right_ref, first_ref, keep_high, keep_low,
    out_ref, resid_ref, inverse_ref, sums_ref, high_ref, low_ref, *stage
):
    vals_ref, tiles, keep = (high_ref, low_ref), (stage[:2], stage[2]), (keep_high, keep_low)
    rows = own_ref.shape[1] // SUP
    groups = group_count(span_ref, rows)
    for g in range(AHEAD):
        fetch(keep, groups, tiles, g, True)
    norm_before, curve_before = frame_columns(first_ref[0:1])[:2]
    alpha = wide(norm_before / curve_before)

    def begin(a, image, values, sums):
        residual = values - alpha * image
        resid_ref[:, lanes(a)] = residual
        return (
            sums[0] + fold(residual * residual), sums[1] + fold(residual * image), larger(sums[2], residual)
        )

    def begin_first(a, sums):
        return begin(a, image_ref[:, lanes(a)] + left_ref[:, lanes(a)], own_ref[:, lanes(a)], sums)

    def begin_rest(a, sums):
        return begin(a, image_ref[:, lanes(a)], own_ref[:, lanes(a)], sums)

    sums = loop(0, HALO, begin_first, (zeros(), zeros(), zeros()))
    norm, cross, peak = loop(HALO, rows, begin_rest, sums)

    def begin_halo(a, peak):
        image = image_ref[:, lanes(rows + a)] + right_ref[:, lanes(a)]
        residual = halo_ref[:, lanes(a)] - alpha * image
        resid_ref[:, lanes(rows + a)] = residual
        return larger(peak, residual)

    scale = scale_of(loop(0, HALO, begin_halo, peak))

    def ready(a, _):
        hold(vals_ref, a, scale * resid_ref[:, lanes(a)])
        return 0

    loop(0, rows + HALO, ready, 0)
    clear(out_ref, 0, rows + HALO)
    sweep_again(span_ref, rows, groups, vals_ref, out_ref, keep, tiles)
    inverse_ref[...] = 1.0 / (KERNEL * scale)
    sums_ref[0], sums_ref[1] = norm, cross


def vals_scratch(count):
    return [
        pltpu.VMEM((count, 2 * FRAMES, SUP), jnp.bfloat16),
        pltpu.VMEM((count, FRAMES, SUP), EIGHT),
    ]


def stage_scratch(slots):
    return [
        pltpu.VMEM((slots, BATCH, SUP, SUP), jnp.bfloat16),
        pltpu.VMEM((slots, BATCH, SUP, SUP), EIGHT),
        pltpu.SemaphoreType.DMA((2, slots)),
    ]


def kept(rows):
    steps = rows // BATCH - (-rows * HALO // BATCH)
    shape = (steps, BATCH, SUP, SUP)
    return jax.ShapeDtypeStruct(shape, jnp.bfloat16), jax.ShapeDtypeStruct(shape, EIGHT)


def first_pass(span, pos, spread, noise, right_side, halo):
    rows = right_side.shape[1] // SUP
    return local_call(
        first_kernel, (span, pos, spread, noise, right_side, halo),
        (f32((FRAMES, (rows + HALO + 1) * SUP)), f32((8, 128))) + kept(rows),
        vals_scratch(rows + HALO) + stage_scratch(2), 1, any_outs=2,
    )


def second_pass(span, noise, right_side, halo, image, left, right, first, keep):
    extent = right_side.shape[1] // SUP + HALO
    return local_call(
        second_kernel, (span, noise, right_side, halo, image, left, right, first, *keep),
        (f32((FRAMES, (extent + 1) * SUP)), f32((FRAMES, extent * SUP)), f32((FRAMES, SUP)), f32((2, FRAMES, 128))),
        vals_scratch(extent) + stage_scratch(AHEAD + 1), 1, anys=2, mib=44,
    )


def local_call(kernel, operands, out_shape, scratch, smalls, anys=0, any_outs=0, mib=32):
    plain = len(operands) - smalls - anys
    return pl.pallas_call(
        kernel,
        out_shape=out_shape,
        in_specs=[SMEM] * smalls + [VMEM] * plain + [ANY] * anys,
        out_specs=(VMEM,) * (len(out_shape) - any_outs) + (ANY,) * any_outs,
        scratch_shapes=scratch,
        compiler_params=pltpu.CompilerParams(vmem_limit_bytes=mib * 2**20),
    )(*operands)


def arrive(peers):
    barrier = pltpu.get_barrier_semaphore()
    for peer in peers:
        pl.semaphore_signal(barrier, inc=1, device_id=(peer,), device_id_type=MESH)
    return lambda: pl.semaphore_wait(barrier, len(peers))


def send(src, dst, sems, index, peer):
    copy = pltpu.make_async_remote_copy(
        src_ref=src, dst_ref=dst, send_sem=sems.at[0, index], recv_sem=sems.at[1, index],
        device_id=(peer,), device_id_type=MESH,
    )
    copy.start()
    return copy


def neighbours():
    size, me = lax.axis_size("pts"), lax.axis_index("pts")
    return lax.rem(me + size - 1, size), lax.rem(me + 1, size)


def partners():
    me = lax.axis_index("pts")
    groups = lax.axis_size("pts") // GROUP
    spot, group = lax.rem(me, GROUP), me // GROUP
    near_peers = [group * GROUP + lax.rem(spot + k, GROUP) for k in range(1, GROUP)]
    far_peers = [lax.rem(group + k, groups) * GROUP + spot for k in range(1, groups)]
    return near_peers, far_peers


def sum_over_devices(total, mine, slots, sems, edges):
    for stage, peers in enumerate(partners()):
        mine[stage, 0:1] = total
        for k, peer in enumerate(peers):
            pltpu.make_async_remote_copy(
                src_ref=mine.at[stage, pl.ds(0, 1)], dst_ref=slots.at[stage, pl.ds(k, 1)],
                send_sem=sems.at[0, stage], recv_sem=sems.at[1, stage], device_id=(peer,), device_id_type=MESH,
            ).start()
        if stage == 0:
            edges()
        rows = slots.at[stage, pl.ds(0, len(peers))]
        for side in range(2):
            pltpu.make_async_copy(rows, rows, sems.at[side, stage]).wait()
        total = total + jnp.sum(slots[stage, 0 : len(peers)], axis=0, keepdims=True)
    return total


def exchange_kernel(
    part_ref, sums_ref, left_out, right_out, total_out, left_buf, right_buf, slots, mine, edge_sems, sems
):
    near_peers, far_peers = partners()
    left, right = neighbours()
    arrive(near_peers + far_peers + [left, right])()
    width = left_buf.shape[1]
    first = part_ref.shape[1] - width - SUP
    copies = []

    def edges():
        copies.append(send(part_ref.at[:, pl.ds(first, width)], left_buf, edge_sems, 0, right))
        copies.append(send(part_ref.at[:, pl.ds(0, width)], right_buf, edge_sems, 1, left))

    total = sum_over_devices(sums_ref[0:1], mine, slots, sems, edges)
    total_out[...] = jnp.broadcast_to(total, (8, 128))
    for copy in copies:
        copy.wait()
    left_out[...] = left_buf[...]
    right_out[...] = right_buf[...]


def finish_kernel(
    part_ref, resid_ref, inverse_ref, norms_ref, noise_ref, image_out, left_out, total_out,
    edge, left_buf, slots, mine, edge_sems, sems
):
    near_peers, far_peers = partners()
    left, right = neighbours()
    arrived = arrive(near_peers + far_peers + [left, right])
    rows = image_out.shape[1] // SUP
    inverse = inverse_ref[...]

    def finish(a, curve):
        at = lanes(a)
        image = part_ref[:, at] * inverse + noise_ref[:, at] * resid_ref[:, at]
        image_out[:, at] = image
        return curve + fold(resid_ref[:, at] * image)

    def finish_halo(a, curve):
        at = lanes(rows + a)
        image = part_ref[:, at] * inverse
        edge[:, lanes(a)] = image
        return curve + fold(resid_ref[:, at] * image)

    curve = loop(0, HALO, finish_halo, loop(0, rows, finish, zeros()))
    total = lane_totals([norms_ref[0], curve, norms_ref[1]])[0:1]
    arrived()
    copies = []
    total = sum_over_devices(
        total, mine, slots, sems, lambda: copies.append(send(edge, left_buf, edge_sems, 0, right))
    )
    total_out[...] = jnp.broadcast_to(total, (8, 128))
    for copy in copies:
        copy.wait()
    left_out[...] = left_buf[...]


def remote_call(kernel, operands, out_shape, scratch, collective_id):
    most = -(-lax.axis_size("pts") // GROUP // 8) * 8
    return pl.pallas_call(
        kernel,
        out_shape=out_shape,
        in_specs=[VMEM] * len(operands),
        out_specs=(VMEM,) * len(out_shape),
        scratch_shapes=scratch
        + [
            pltpu.VMEM((2, most, 128), jnp.float32),
            pltpu.VMEM((2, 8, 128), jnp.float32),
            pltpu.SemaphoreType.DMA((2, 2)),
            pltpu.SemaphoreType.DMA((2, 2)),
        ],
        compiler_params=pltpu.CompilerParams(
            collective_id=collective_id, has_side_effects=True, vmem_limit_bytes=16 * 2**20
        ),
    )(*operands)


def last_kernel(
    own_ref, image_ref, left_ref, part_ref, left2_ref, first_ref, second_ref, field_out, resid_out, field_ref, resid_ref, sems
):
    norm0, curve0 = frame_columns(first_ref[0:1])[:2]
    norm1, curve1, cross1 = frame_columns(second_ref[0:1])[:3]
    beta = norm1 / norm0
    alpha0 = wide(norm0 / curve0)
    alpha1 = wide(norm1 / (curve1 + 2.0 * beta * cross1 + beta * beta * curve0))
    beta = wide(beta)
    width = HALO * SUP
    copies = []
    for part in range(own_ref.shape[1] // width):
        def step(a, _):
            at = lanes(part * HALO + a)
            first, image, image_next = own_ref[:, at], image_ref[:, at], part_ref[:, at]
            if part == 0:
                image = image + left_ref[:, at]
                image_next = image_next + left2_ref[:, at]
            residual = first - alpha0 * image
            direction = residual + beta * first
            field_ref[:, at] = alpha0 * first + alpha1 * direction
            resid_ref[:, at] = residual - alpha1 * (image_next + beta * image)
            return 0

        loop(0, HALO, step, 0)
        at = pl.ds(part * width, width)
        for index, (src, dst) in enumerate(((field_ref, field_out), (resid_ref, resid_out))):
            copies.append(pltpu.make_async_copy(src.at[:, at], dst.at[:, at], sems.at[index, part]))
            copies[-1].start()
    for copy in copies:
        copy.wait()


def spans(boxes, rows, limit):
    low, high = boxes
    lane = lax.broadcasted_iota(jnp.int32, (1, 128), 1)
    span = jnp.zeros((1, 128), jnp.int32)
    for k in range(1, HALO + 1):
        low_k, high_k = pltpu.roll(low, 128 - k, 1), pltpu.roll(high, 128 - k, 1)
        gap = jnp.maximum(jnp.maximum(low_k - high, low - high_k), 0.0)
        near = (jnp.sum(gap * gap, axis=0, keepdims=True) < UNIT * UNIT) & (lane + k < limit)
        span = jnp.where(near, k, span)
    return jnp.broadcast_to(jnp.where(lane < rows, span, 0), (8, 128))


def start_kernel(
    positions_any, own_any, pos_ref, halo_ref, span_ref, rows_ref, own_out, positions_ref, edge_pos, edge, local_sems, sems
):
    rows = own_any.shape[1] // SUP
    width = HALO * SUP
    size = lax.axis_size("pts")
    me = lax.axis_index("pts")
    right, left = lax.rem(me + 1, size), lax.rem(me + size - 1, size)
    barrier = pltpu.get_barrier_semaphore()
    for peer in (left, right):
        pl.semaphore_signal(barrier, inc=1, device_id=(peer,), device_id_type=MESH)
    bring = pltpu.make_async_copy(positions_any, positions_ref, local_sems.at[0])
    bring.start()
    pass_on = pltpu.make_async_copy(own_any, own_out, local_sems.at[1])
    pass_on.start()
    pl.semaphore_wait(barrier, 2)
    copies = []
    for index, (src, dst) in enumerate(((positions_any, edge_pos), (own_any, edge))):
        copies.append(
            pltpu.make_async_remote_copy(
                src_ref=src.at[:, pl.ds(0, width)], dst_ref=dst, send_sem=sems.at[0, index], recv_sem=sems.at[1, index],
                device_id=(left,), device_id_type=MESH,
            )
        )
        copies[-1].start()
    bring.wait()
    blank = jnp.zeros((5, width), jnp.float32)
    for part in range(rows // HALO):
        at = slice(part * width, (part + 1) * width)
        pos_ref[:, at] = jnp.concatenate([UNIT * positions_ref[:, at], blank], axis=0)
    lane = lax.broadcasted_iota(jnp.int32, (8, 128), 1)

    def box(a, boxes):
        points = pos_ref[:, lanes(a)]
        low = jnp.min(jnp.minimum(points[:, :128], points[:, 128:]), axis=1, keepdims=True)
        high = jnp.max(jnp.maximum(points[:, :128], points[:, 128:]), axis=1, keepdims=True)
        return jnp.where(lane == a, low, boxes[0]), jnp.where(lane == a, high, boxes[1])

    none = jnp.zeros((8, 128), jnp.float32)
    boxes = loop(0, rows, box, (none, none))
    spread_rows(pos_ref, rows_ref, rows)
    for copy in copies:
        copy.wait()
    pass_on.wait()
    pos_ref[:, rows * SUP :] = jnp.concatenate([UNIT * edge_pos[...], blank], axis=0)
    halo_ref[...] = edge[...]
    boxes = loop(rows, rows + HALO, box, boxes)
    span_ref[...] = spans(boxes, rows, jnp.where(me == size - 1, rows, rows + HALO))


def start(positions, right_side, collective_id):
    rows = right_side.shape[1] // SUP
    width = HALO * SUP
    return pl.pallas_call(
        start_kernel,
        out_shape=(
            f32((8, (rows + HALO) * SUP)), f32((FRAMES, width)), jax.ShapeDtypeStruct((8, 128), jnp.int32),
            f32((rows, 3, SUP, 128)), f32(right_side.shape),
        ),
        in_specs=[ANY, VMEM],
        out_specs=(VMEM,) * 5,
        scratch_shapes=[
            pltpu.VMEM(positions.shape, jnp.float32),
            pltpu.VMEM((3, width), jnp.float32),
            pltpu.VMEM((FRAMES, width), jnp.float32),
            pltpu.SemaphoreType.DMA((2,)),
            pltpu.SemaphoreType.DMA((2, 2)),
        ],
        compiler_params=pltpu.CompilerParams(
            collective_id=collective_id, has_side_effects=True, vmem_limit_bytes=28 * 2**20
        ),
    )(positions, right_side)


def body(positions, noise, right_side, pairs, counts):
    rows = positions.shape[1] // SUP
    noise = noise.reshape(1, -1)
    pos, halo, span, spread, right_side = start(positions, right_side, 2)
    image, sums, *keep = first_pass(span, pos, spread, noise, right_side, halo)
    edge = f32(halo.shape)
    held = pltpu.VMEM(halo.shape, jnp.float32)
    left, right, first = remote_call(exchange_kernel, (image, sums), (edge, edge, f32((8, 128))), [held] * 2, 0)
    part, resid, inverse, norms = second_pass(span, noise, right_side, halo, image, left, right, first, keep)
    part, left2, second = remote_call(
        finish_kernel, (part, resid, inverse, norms, noise), (f32(right_side.shape), edge, f32((8, 128))), [held] * 2, 1
    )
    parts = rows // HALO
    return local_call(
        last_kernel, (right_side, image, left, part, left2, first, second),
        (f32(right_side.shape), f32(right_side.shape)),
        [pltpu.VMEM(right_side.shape, jnp.float32)] * 2 + [pltpu.SemaphoreType.DMA((2, parts))], 0, any_outs=2,
    )


def solution(mesh):
    in_specs = (P(None, "pts"), P("pts"), P(None, "pts"), P(None, "pts"), P("pts"))
    out_specs = (P(None, "pts"), P(None, "pts"))
    return jax.shard_map(body, mesh=mesh, in_specs=in_specs, out_specs=out_specs, check_vma=False)
```
